128 devices in a mesh: tm: 16 (over y_lo, x, core), row: 8 (over z, y_hi).
Axes of the slice: x: 4, y: 4 (y_hi: 2, y_lo: 2; y = y_hi * 2 + y_lo), z: 4, core: 2. Of those that a mesh axis runs over, the one named last changes fastest.
Arguments:
- feature: bfloat16 [64, 32, 128, 384], P('tm', 'row'), may hold values from -6 to 6
- conv_weight: bfloat16 [3, 3, 3, 384, 384], replicated, may hold values from -0.0625 to 0.0625
- conv_bias: float32 [384], replicated, may hold values from -3 to 3
- down_weight: bfloat16 [3, 2, 2, 384, 16], replicated, may hold values from -0.09375 to 0.09375
- down_bias: float32 [16], replicated, may hold values from -3 to 3
Outputs:
- tokens: float32 [8192, 64], P(('tm', 'row'))
The draws below stay inside these ranges and needn't reach their ends.
All inputs are finite; a program needn't handle non-finite values.
Results may differ from the reference program's by a relative error of at most 0.0022.
Values may be sent and summed in bfloat16 or wider, within the bound.
No kernel may reach another device: no remote copies, remote signals or barrier semaphores. Data moves between devices by JAX's collectives and lax.ppermute only.
A program may use at most 128 MiB of HBM per device.

```python
import jax
import jax.numpy as jnp
from jax import lax

C = 384
Z = 16
LW = 64
TLAT = 32
HL = 16
TIN = 64
HIN = 32
WIN = 128
TOKENS = 8192


def shard_levels(own_key, extent, cuts, smallest, top_value):
    gain, own = 1.0, jax.random.fold_in(own_key, 6)
    for dim, parts in cuts:
        steps = jnp.exp(jax.random.uniform(jax.random.fold_in(own, dim), (parts,), jnp.float32, smallest / len(cuts), top_value / len(cuts)))
        gain = gain * jnp.repeat(steps, extent[dim] // parts).reshape([-1 if axis == dim else 1 for axis in range(len(extent))])
    return gain


def gaussian(rng, extent, width, most, split=(), kind=jnp.bfloat16):
    drawn = jax.random.normal(rng, extent, jnp.float32) * width
    if len(split) > 0:
        drawn = shard_levels(rng, extent, split, -0.22, 0.18) * drawn
    return jnp.clip(drawn, min=-most, max=most).astype(kind)


def setup_inputs(seed: int = 0) -> dict:
    arg_keys = jax.random.split(jax.random.key(seed), 6)
    feature = gaussian(arg_keys[0], (TIN, HIN, WIN, C), 1.0, 6.0, ((0, 16), (1, 8)))
    conv_weight = gaussian(arg_keys[1], (3, 3, 3, C, C), (27 * C) ** -0.5, 0.0625)
    conv_bias = gaussian(arg_keys[2], (C,), 0.5, 3.0, (), jnp.float32)
    down_weight = gaussian(arg_keys[3], (3, 2, 2, C, Z), (12 * C) ** -0.5, 0.09375)
    down_bias = gaussian(arg_keys[4], (Z,), 0.5, 3.0, (), jnp.float32)
    return dict(feature=feature, conv_weight=conv_weight, conv_bias=conv_bias, down_weight=down_weight, down_bias=down_bias)


def reference(feature, conv_weight, conv_bias, down_weight, down_bias):
    channels = feature.shape[-1]
    padded = jnp.pad(feature, ((2, 0), (1, 1), (1, 1), (0, 0)))
    kernel = conv_weight.astype(jnp.float32).reshape(27 * channels, channels)

    def one_frame(frame):
        window = lax.dynamic_slice_in_dim(padded, frame, 3, 0)
        pieces = []
        for tap_time in range(3):
            for tap_row in range(3):
                for tap_col in range(3):
                    pieces.append(window[tap_time, tap_row:tap_row + HIN, tap_col:tap_col + WIN, :])
        columns = jnp.concatenate(pieces, axis=-1).astype(jnp.float32).reshape(HIN * WIN, 27 * channels)
        pre = jnp.dot(columns, kernel, precision=lax.Precision.HIGHEST) + conv_bias
        return jax.nn.silu(pre).astype(jnp.bfloat16).reshape(HIN, WIN, channels)

    act = lax.map(one_frame, jnp.arange(TIN, dtype=jnp.int32))
    shifted = jnp.concatenate([jnp.zeros((1, HIN, WIN, channels), jnp.bfloat16), act], axis=0)
    slabs = []
    for tap_time in range(3):
        part = shifted[tap_time:tap_time + 2 * TLAT:2]
        part = part.reshape(TLAT, HL, 2, LW, 2, channels).transpose(0, 1, 3, 2, 4, 5)
        slabs.append(part.reshape(TLAT * HL * LW, 4 * channels))
    stacked = jnp.concatenate(slabs, axis=-1).astype(jnp.float32)
    down = down_weight.astype(jnp.float32).reshape(12 * channels, Z)
    latent = jnp.dot(stacked, down, precision=lax.Precision.HIGHEST) + down_bias
    latent = latent.reshape(TLAT, HL // 2, 2, LW // 2, 2, Z).transpose(0, 1, 3, 2, 4, 5)
    return latent.reshape(TOKENS, 4 * Z)
```

```python
import jax
import jax.numpy as jnp
from jax import lax
from jax.experimental import pallas as pl
from jax.experimental.pallas import tpu as pltpu
from jax.sharding import PartitionSpec as P

F32 = jnp.float32
BF16 = jnp.bfloat16
VMEM_LIMIT = 48 * 1024 * 1024


def widen(rows, store, width, channels):
    value = rows.astype(F32)
    column = lax.broadcasted_iota(jnp.int32, (width, channels), 0)
    before = jnp.where(column == 0, 0.0, pltpu.roll(value, 1, 0))
    after = jnp.where(column == width - 1, 0.0, pltpu.roll(value, width - 1, 0))
    store(slice(0, channels), before.astype(BF16))
    store(slice(channels, 2 * channels), rows)
    store(slice(2 * channels, 3 * channels), after.astype(BF16))


def silu(pre):
    return pre / (1.0 + jnp.exp(-pre))


def token_rows(product, d_ref, half, i):
    d_ref[half] = product
    count = product.shape[0] // 4
    lane = lax.broadcasted_iota(jnp.int32, (count, 128), 1)
    right_row = (lane // 32) % 2 == i // 2
    total = jnp.zeros((count, 128), F32)
    for s in range(4):
        keep = right_row & (lane // 64 == s % 2) & ((lane // 16) % 2 == s // 2)
        total = total + jnp.where(keep, d_ref[half, pl.ds(s, count, stride=4), :], 0.0)
    return total


def project(pre, bias_ref, even_ref, odd_ref, d_ref, f, i):
    act = silu(pre + bias_ref[...]).astype(BF16)
    if f % 2 == 0:
        product = jnp.dot(act, even_ref[i % 2], preferred_element_type=F32)
        return token_rows(product, d_ref, 0, i), None
    product = jnp.dot(act, odd_ref[i % 2], preferred_element_type=F32)
    return token_rows(product[:, :128], d_ref, 0, i), token_rows(product[:, 128:], d_ref, 1, i)


def own_kernel(x_ref, w_ref, bias_ref, even_ref, odd_ref, early_ref, edge_ref, tok_ref, acc, wide, d_ref):
    step = pl.program_id(0)
    frames, height, width, channels = x_ref.shape
    tap_time = 2 - step // 3

    @pl.when(step == 0)
    def _():
        def one(n, carry):
            f, h = n // height, n % height

            def store(lanes, value):
                wide[f, h, :, lanes] = value

            widen(x_ref[f, h], store, width, channels)
            return carry

        lax.fori_loop(0, frames * height, one, 0)

    def tap(first, count, shift, init):
        weight = w_ref[0, 0].reshape(3 * channels, channels)

        def one(g, carry):
            left = wide[g, first : first + count].reshape(count * width, 3 * channels)
            product = jnp.dot(left, weight, preferred_element_type=F32).reshape(count, width, channels)
            target = (g + 2 - tap_time, slice(first + shift, first + shift + count))
            if init:
                acc[target] = product
            else:
                acc[target] += product
            return carry

        lax.fori_loop(0, frames - 2 + tap_time, one, 0)

    pl.when(step == 0)(lambda: tap(0, height, 0, True))
    pl.when((step % 3 == 0) & (step > 0))(lambda: tap(0, height, 0, False))
    pl.when(step % 3 == 1)(lambda: tap(0, height - 1, 1, False))
    pl.when(step % 3 == 2)(lambda: tap(1, height - 1, -1, False))

    @pl.when(step == 8)
    def _():
        early_ref[...] = acc[:2]
        for side, i in enumerate((0, height - 1)):
            for f in (2, 3):
                edge_ref[f - 2, side] = acc[f, i]
        late = jnp.zeros((width // 4, 128), F32)
        coming = jnp.zeros((width // 4, 128), F32)
        for i in range(1, height - 1):
            for f in (2, 3):
                main, other = project(acc[f, i], bias_ref, even_ref, odd_ref, d_ref, f, i)
                late = late + main
                if other is not None:
                    coming = coming + other
        tok_ref[0] = late
        tok_ref[1] = coming


def earlier_kernel(x_ref, early_in, w_ref, bias_ref, even_ref, odd_ref, edge_ref, tok_ref, acc, wide, d_ref):
    step = pl.program_id(0)
    frames, height, width, channels = x_ref.shape
    tap_time = step // 3

    @pl.when(step == 0)
    def _():
        def one(n, carry):
            f, h = n // height, n % height

            def store(lanes, value):
                wide[f, h, :, lanes] = value

            widen(x_ref[f, h], store, width, channels)
            return carry

        lax.fori_loop(0, frames * height, one, 0)
        acc[...] = early_in[...]

    def tap(first, count, shift):
        weight = w_ref[0, 0].reshape(3 * channels, channels)

        def one(f, carry):
            left = wide[f + tap_time, first : first + count].reshape(count * width, 3 * channels)
            product = jnp.dot(left, weight, preferred_element_type=F32).reshape(count, width, channels)
            acc[f, first + shift : first + shift + count] += product
            return carry

        lax.fori_loop(0, 2 - tap_time, one, 0)

    pl.when(step % 3 == 0)(lambda: tap(0, height, 0))
    pl.when(step % 3 == 1)(lambda: tap(0, height - 1, 1))
    pl.when(step % 3 == 2)(lambda: tap(1, height - 1, -1))

    @pl.when(step == 5)
    def _():
        for side, i in enumerate((0, height - 1)):
            for f in (0, 1):
                edge_ref[f, side] = acc[f, i]
        first = jnp.zeros((width // 4, 128), F32)
        late = jnp.zeros((width // 4, 128), F32)
        for i in range(1, height - 1):
            for f in (0, 1):
                main, other = project(acc[f, i], bias_ref, even_ref, odd_ref, d_ref, f, i)
                first = first + main
                if other is not None:
                    late = late + other
        tok_ref[0] = first
        tok_ref[1] = late


def edge_kernel(
    odd_row_ref, up23, dn23, up01, dn01, corner, edge01, edge23, tok_a, tok_b, w_ref, bias_ref, even_ref, odd_ref,
    down_bias_ref, out_ref, acc, wide, d_ref,
):
    step = pl.program_id(0)
    width, channels = up23.shape[2:]
    tap_time = step // 2

    @pl.when(step == 0)
    def _():
        for side in range(2):
            sources = [corner.at[0, side], corner.at[1, side]]
            sources += [(up01, dn01)[side].at[f, 0] for f in range(2)]
            sources += [(up23, dn23)[side].at[f, 0] for f in range(2)]
            for n, source in enumerate(sources):

                def store(lanes, value):
                    wide[side, n, :, lanes] = value

                widen(source[...], store, width, channels)
            for f in range(2):
                acc[side, f] = edge01[f, side]
                acc[side, f + 2] = edge23[f, side]

    def tap(side):
        weight = w_ref[0, 0].reshape(3 * channels, channels)
        left = wide[side, pl.ds(tap_time, 4)].reshape(4 * width, 3 * channels)
        acc[side] += jnp.dot(left, weight, preferred_element_type=F32).reshape(4, width, channels)

    pl.when(step % 2 == 0)(lambda: tap(0))
    pl.when(step % 2 == 1)(lambda: tap(1))

    @pl.when(step == 5)
    def _():
        first = tok_b[0]
        late = tok_a[0] + tok_b[1]
        coming = tok_a[1]
        for side, i in enumerate((0, 3)):
            for f in range(4):
                main, other = project(acc[side, f], bias_ref, even_ref, odd_ref, d_ref, f, i)
                if f < 2:
                    first = first + main
                else:
                    late = late + main
                if f == 1:
                    late = late + other
                if f == 3:
                    coming = coming + other

        def fold(value):
            return (value + pltpu.roll(value, 64, 1))[:, :64]

        first = fold(first) + down_bias_ref[...]
        late = fold(late) + down_bias_ref[...]
        odd = odd_row_ref[0] == 1
        out_ref[0] = jnp.where(odd, late, first)
        out_ref[1] = jnp.where(odd, first, late)
        out_ref[2] = fold(coming)


def whole(shape):
    return pl.BlockSpec(shape, lambda s: (0,) * len(shape))


def params():
    return pltpu.CompilerParams(vmem_limit_bytes=VMEM_LIMIT, dimension_semantics=("arbitrary",))


def cost(units, width, channels):
    return pl.CostEstimate(flops=units * width * 3 * channels * channels * 2, bytes_accessed=10_000_000, transcendentals=0)


def on_device(feature, conv_weight, conv_bias, down_weight, down_bias):
    frames, height, width, channels = feature.shape
    z = down_bias.shape[0]
    n_tm, n_row = lax.axis_size("tm"), lax.axis_size("row")
    axes = ("tm", "row")

    def shifted(value, by_tm, by_row):
        pairs = [
            (t * n_row + r, (t + by_tm) * n_row + r + by_row)
            for t in range(n_tm)
            for r in range(n_row)
            if 0 <= t + by_tm < n_tm and 0 <= r + by_row < n_row
        ]
        return lax.ppermute(value, axes, pairs)

    up23 = shifted(feature[2:, height - 1 :], 0, 1)
    dn23 = shifted(feature[2:, :1], 0, -1)
    earlier = shifted(feature[2:], 1, 0)
    up01 = shifted(feature[:2, height - 1 :], 0, 1)
    dn01 = shifted(feature[:2, :1], 0, -1)
    corner = shifted(jnp.concatenate([up23, dn23], axis=1), 1, 0)

    spread = jnp.broadcast_to(
        down_weight.transpose(0, 1, 3, 2, 4)[:, :, :, :, None, :], (3, 2, channels, 2, 4, z)
    ).reshape(3, 2, channels, 8 * z)
    even = spread[1]
    odd = jnp.concatenate([spread[2], spread[0]], axis=-1)
    bias = conv_bias.reshape(1, channels)
    patch_bias = jnp.tile(down_bias, 4).reshape(1, 4 * z)
    quarter = width // 4
    lanes = 8 * z
    tok = jax.ShapeDtypeStruct((2, quarter, lanes), F32)
    edges = jax.ShapeDtypeStruct((2, 2, width, channels), F32)
    early_shape = jax.ShapeDtypeStruct((2, height, width, channels), F32)

    def weight_spec(where):
        return pl.BlockSpec((1, 1, 3, channels, channels), lambda s: where(s) + (0, 0, 0))

    small = [whole((1, channels)), whole((2, channels, lanes)), whole((2, channels, 2 * lanes))]
    early, edge23, tok_a = pl.pallas_call(
        own_kernel,
        grid=(9,),
        in_specs=[whole(feature.shape), weight_spec(lambda s: (2 - s // 3, (1 + 2 * (s % 3)) % 3)), *small],
        out_specs=[whole(early_shape.shape), whole(edges.shape), whole(tok.shape)],
        out_shape=[early_shape, edges, tok],
        scratch_shapes=[
            pltpu.VMEM((frames, height, width, channels), F32),
            pltpu.VMEM((frames, height, width, 3 * channels), BF16),
            pltpu.VMEM((2, width, 128), F32),
        ],
        compiler_params=params(),
        cost_estimate=cost(90, width, channels),
        name="own",
    )(feature, conv_weight, bias, even, odd)
    edge01, tok_b = pl.pallas_call(
        earlier_kernel,
        grid=(6,),
        in_specs=[
            whole(earlier.shape), whole(early_shape.shape),
            weight_spec(lambda s: (s // 3, (1 + 2 * (s % 3)) % 3)), *small,
        ],
        out_specs=[whole(edges.shape), whole(tok.shape)],
        out_shape=[edges, tok],
        scratch_shapes=[
            pltpu.VMEM((2, height, width, channels), F32),
            pltpu.VMEM((2, height, width, 3 * channels), BF16),
            pltpu.VMEM((2, width, 128), F32),
        ],
        compiler_params=params(),
        cost_estimate=cost(30, width, channels),
        name="earlier",
    )(earlier, early, conv_weight, bias, even, odd)
    row = lax.axis_index("row")
    odd_row = (row % 2).reshape(1).astype(jnp.int32)
    halo = (2, 1, width, channels)
    out = pl.pallas_call(
        edge_kernel,
        grid=(6,),
        in_specs=[
            pl.BlockSpec(memory_space=pltpu.SMEM),
            whole(halo), whole(halo), whole(halo), whole(halo), whole(corner.shape),
            whole(edges.shape), whole(edges.shape), whole(tok.shape), whole(tok.shape),
            weight_spec(lambda s: (s // 2, 2 * (s % 2))), *small, whole((1, 4 * z)),
        ],
        out_specs=whole((3, quarter, 4 * z)),
        out_shape=jax.ShapeDtypeStruct((3, quarter, 4 * z), F32),
        scratch_shapes=[
            pltpu.VMEM((2, frames, width, channels), F32),
            pltpu.VMEM((2, frames + 2, width, 3 * channels), BF16),
            pltpu.VMEM((2, width, 128), F32),
        ],
        compiler_params=params(),
        cost_estimate=cost(24, width, channels),
        name="edges",
    )(odd_row, up23, dn23, up01, dn01, corner, edge01, edge23, tok_a, tok_b, conv_weight, bias, even, odd, patch_bias)

    half = n_row // 2

    def routed(value, by_tm, slot, rows):
        pairs = []
        for t in range(n_tm - by_tm):
            for r in rows:
                first = (r % 2 == 0) == (slot == 0)
                target = r // 2 if by_tm or first else half + r // 2
                pairs.append((t * n_row + r, (t + by_tm) * n_row + target))
        return lax.ppermute(value, axes, pairs)

    got_a = routed(out[0], 0, 0, range(n_row))
    got_b = routed(out[1], 0, 1, range(n_row))
    prev_even = routed(out[2], 1, 0, range(0, n_row, 2))
    prev_odd = routed(out[2], 1, 0, range(1, n_row, 2))
    low = row < half
    return jnp.concatenate(
        [jnp.where(low, got_a, got_b) + prev_even, jnp.where(low, got_b, got_a) + prev_odd], axis=0
    )


def solution(mesh):
    return jax.shard_map(
        on_device,
        mesh=mesh,
        in_specs=(P("tm", "row", None, None), P(), P(), P(), P()),
        out_specs=P(("tm", "row"), None),
        check_vma=False,
    )
```

```python
import jax
import jax.numpy as jnp
from jax import lax
from jax.experimental import pallas as pl
from jax.experimental.pallas import tpu as pltpu
from jax.sharding import PartitionSpec as P

F32 = jnp.float32
BF16 = jnp.bfloat16
VMEM_LIMIT = 28 * 1024 * 1024
AXES = ("tm", "row")


def widen(rows, target, keep=None):
    width, channels = rows.shape
    if keep is not None:
        rows = jnp.where(keep, rows.astype(F32), 0.0).astype(BF16)
    value = rows.astype(F32)
    column = lax.broadcasted_iota(jnp.int32, (width, channels), 0)
    before = jnp.where(column == 0, 0.0, pltpu.roll(value, 1, 0))
    after = jnp.where(column == width - 1, 0.0, pltpu.roll(value, width - 1, 0))
    target[:, 0:channels] = before.astype(BF16)
    target[:, channels : 2 * channels] = rows
    target[:, 2 * channels : 3 * channels] = after.astype(BF16)


def tap_product(w_ref, positions):
    channels = w_ref.shape[-1]
    weight = w_ref[0, 0].reshape(3 * channels, channels)
    positions = positions.reshape(-1, 3 * channels)
    return lax.dot_general(weight, positions, (((0,), (1,)), ((), ())), preferred_element_type=F32)


def projected(pre, bias, down_ref, f, rows):
    taps = (1,) if f % 2 == 0 else (2, 0)
    act = []
    for value in pre:
        value = value + bias
        act.append((value / (1.0 + jnp.exp(-value))).astype(BF16))
    weight = []
    for a in taps:
        for i in rows:
            parts = [down_ref[a, i % 2, dx] for dx in (0, 0, 1, 1)]
            weight.append(jnp.concatenate(parts, axis=0))
    product = jnp.dot(jnp.concatenate(weight, axis=0), jnp.concatenate(act, axis=1), preferred_element_type=F32)
    width = pre[0].shape[1]
    size = weight[0].shape[0]
    found = {}
    for n, a in enumerate(taps):
        for half in range(2):
            first = (2 * n + half) * size
            found[a, half] = product[first : first + size, half * width : (half + 1) * width]
    return found


def add_products(found, a, total_ref):
    for half in range(2):
        value = found[a, half]
        size = value.shape[0] // 2
        for dx in range(2):
            first = dx * 2 * size + half * size
            total_ref[first : first + size, :] += value[dx * size : (dx + 1) * size]


def fold(total, d_ref):
    d_ref[...] = total.T
    lanes = total.shape[0]
    count = total.shape[1] // 4
    lane = lax.broadcasted_iota(jnp.int32, (count, lanes), 1)
    result = jnp.zeros((count, lanes), F32)
    for s in range(4):
        keep = (lane // (lanes // 2) == s % 2) & ((lane // (lanes // 8)) % 2 == s // 2)
        result = result + jnp.where(keep, d_ref[pl.ds(s, count, stride=4), :], 0.0)
    return (result + pltpu.roll(result, lanes // 2, 1))[:, : lanes // 2]


def bias_columns(bias_ref, width):
    return jnp.broadcast_to(bias_ref[...], (width, bias_ref.shape[1])).T


def own_kernel(x_ref, w_ref, bias_ref, down_ref, early_ref, edge_ref, total_ref, acc, wide):
    step = pl.program_id(0)
    frames, height, width, channels = x_ref.shape

    @pl.when(step == 0)
    def _():
        def one(n, carry):
            f, h = n // height, n % height
            widen(x_ref[f, h], wide.at[h, f])
            return carry

        lax.fori_loop(0, frames * height, one, 0)

    def tap(n):
        tap_time, tap_row = 2 - n // 3, (1 + 2 * (n % 3)) % 3
        count = frames - 2 + tap_time
        rows = range(max(0, tap_row - 1), min(height, height + tap_row - 1))
        product = tap_product(w_ref, wide[rows[0] : rows[-1] + 1, :count])
        for m, h in enumerate(rows):
            for g in range(count):
                first = (m * count + g) * width
                value = product[:, first : first + width]
                target = (h + 1 - tap_row, g + 2 - tap_time)
                if n == 0:
                    acc[target] = value
                else:
                    acc[target] += value

    for n in range(9):
        pl.when(step == n)(lambda n=n: tap(n))

    @pl.when(step == 8)
    def _():
        early_ref[...] = acc[:, :2]
        for side, i in enumerate((0, height - 1)):
            for f in (2, 3):
                edge_ref[side, f - 2] = acc[i, f]
        bias = bias_columns(bias_ref, width)
        total_ref[...] = jnp.zeros_like(total_ref)
        for f in (2, 3):
            found = projected([acc[1, f], acc[2, f]], bias, down_ref, f, (1, 2))
            add_products(found, 2 - (f + 1) % 2, total_ref.at[0])
            if f == 3:
                add_products(found, 0, total_ref.at[1])


def earlier_kernel(flag_ref, x_ref, early_in, w_ref, bias_ref, down_ref, edge_ref, total_ref, acc, wide):
    step = pl.program_id(0)
    frames, height, width, channels = x_ref.shape

    @pl.when(step == 0)
    def _():
        keep = flag_ref[2] == 1

        def one(n, carry):
            f, h = n // height, n % height
            widen(x_ref[f, h], wide.at[h, f], keep)
            return carry

        lax.fori_loop(0, frames * height, one, 0)

    def tap(n):
        tap_time, tap_row = n // 3, (1 + 2 * (n % 3)) % 3
        rows = range(max(0, tap_row - 1), min(height, height + tap_row - 1))
        count = frames - tap_time
        product = tap_product(w_ref, wide[rows[0] : rows[-1] + 1, tap_time:])
        for m, h in enumerate(rows):
            for f in range(count):
                first = (m * count + f) * width
                value = product[:, first : first + width]
                target = (h + 1 - tap_row, f)
                if n == 0:
                    acc[target] = early_in[target] + value
                else:
                    acc[target] += value

    for n in range(6):
        pl.when(step == n)(lambda n=n: tap(n))

    @pl.when(step == 5)
    def _():
        for side, i in enumerate((0, height - 1)):
            for f in (0, 1):
                edge_ref[side, f] = acc[i, f]
        bias = bias_columns(bias_ref, width)
        total_ref[...] = jnp.zeros_like(total_ref)
        for f in (0, 1):
            found = projected([acc[1, f], acc[2, f]], bias, down_ref, f, (1, 2))
            add_products(found, 2 - (f + 1) % 2, total_ref.at[0])
            if f == 1:
                add_products(found, 0, total_ref.at[1])


def edge_taps(sources, edge_in, w_ref, acc, wide):
    step = pl.program_id(0)

    @pl.when(step == 0)
    def _():
        for side in range(2):
            for n, (source, keep) in enumerate(sources[side]):
                widen(source[...], wide.at[side, n], keep)

    def tap(n):
        tap_time, side = n // 2, n % 2
        product = tap_product(w_ref, wide[side, tap_time : tap_time + 2])
        width = product.shape[1] // 2
        for f in range(2):
            value = product[:, f * width : (f + 1) * width]
            if tap_time == 0:
                acc[side, f] = edge_in[side, f] + value
            else:
                acc[side, f] += value

    for n in range(6):
        pl.when(step == n)(lambda n=n: tap(n))


def late_edge_kernel(flag_ref, up, dn, edge_in, total_in, w_ref, bias_ref, down_ref, late_ref, carry_ref, acc, wide, total, d_ref):
    flags = [flag_ref[side] == 1 for side in range(2)]
    edge_taps([[(ref.at[f, 0], flags[side]) for f in range(4)] for side, ref in enumerate((up, dn))], edge_in, w_ref, acc, wide)

    @pl.when(pl.program_id(0) == 5)
    def _():
        bias = bias_columns(bias_ref, acc.shape[-1])
        total[...] = total_in[...]
        for f in (0, 1):
            found = projected([acc[0, f], acc[1, f]], bias, down_ref, f, (0, 3))
            add_products(found, 2 - (f + 1) % 2, total.at[0])
            if f == 1:
                add_products(found, 0, total.at[1])
        late_ref[...] = total[0]
        carry_ref[...] = fold(total[1], d_ref)


def early_edge_kernel(
    flag_ref, up, dn, corner, edge_in, total_in, late_in, w_ref, bias_ref, down_ref, down_bias_ref, out_ref, acc, wide, total, d_ref
):
    flags = [flag_ref[side] == 1 for side in range(2)]
    before = [flag & (flag_ref[2] == 1) for flag in flags]
    edge_taps(
        [
            [(corner.at[f, side], before[side]) for f in range(2)] + [(ref.at[f, 0], flags[side]) for f in range(2)]
            for side, ref in enumerate((up, dn))
        ],
        edge_in, w_ref, acc, wide,
    )

    @pl.when(pl.program_id(0) == 5)
    def _():
        bias = bias_columns(bias_ref, acc.shape[-1])
        total[...] = total_in[...]
        for f in (0, 1):
            found = projected([acc[0, f], acc[1, f]], bias, down_ref, f, (0, 3))
            add_products(found, 2 - (f + 1) % 2, total.at[0])
            if f == 1:
                add_products(found, 0, total.at[1])
        out_ref[0] = fold(total[0], d_ref) + down_bias_ref[...]
        out_ref[1] = fold(total[1] + late_in[...], d_ref) + down_bias_ref[...]


def whole(shape):
    return pl.BlockSpec(tuple(shape), lambda s: (0,) * len(shape))


def on_device(feature, conv_weight, conv_bias, down_weight, down_bias):
    frames, height, width, channels = feature.shape
    z = down_bias.shape[0]
    n_tm, n_row = lax.axis_size("tm"), lax.axis_size("row")
    tm, row = lax.axis_index("tm"), lax.axis_index("row")
    quarter, lanes = width // 4, 8 * z

    def shifted(value, by_tm, by_row):
        pairs = [
            (t * n_row + r, (t + by_tm) % n_tm * n_row + (r + by_row) % n_row) for t in range(n_tm) for r in range(n_row)
        ]
        return lax.ppermute(value, AXES, pairs)

    flags = jnp.stack([row > 0, row < n_row - 1, tm > 0]).astype(jnp.int32)
    up = shifted(feature[:, height - 1 :], 0, 1)
    dn = shifted(feature[:, :1], 0, -1)
    earlier = shifted(feature[2:], 1, 0)

    bias = conv_bias.reshape(1, channels)
    down = down_weight.transpose(0, 1, 2, 4, 3)
    patch_bias = jnp.tile(down_bias, 4).reshape(1, 4 * z)
    edges = jax.ShapeDtypeStruct((2, 2, channels, width), F32)
    totals = jax.ShapeDtypeStruct((2, lanes, width), F32)
    early_shape = jax.ShapeDtypeStruct((height, 2, channels, width), F32)
    flag_spec = pl.BlockSpec(memory_space=pltpu.SMEM)

    def weights(where):
        return [
            pl.BlockSpec((1, 1, 3, channels, channels), lambda s: where(s) + (0, 0, 0)), whole(bias.shape), whole(down.shape)
        ]

    def call(kernel, name, steps, units, ins, specs, outs, scratch):
        return pl.pallas_call(
            kernel,
            grid=(steps,),
            in_specs=specs,
            out_specs=[whole(o.shape) for o in outs],
            out_shape=outs,
            scratch_shapes=scratch,
            compiler_params=pltpu.CompilerParams(vmem_limit_bytes=VMEM_LIMIT, dimension_semantics=("arbitrary",)),
            cost_estimate=pl.CostEstimate(
                flops=units * width * 6 * channels * channels, bytes_accessed=10_000_000, transcendentals=0
            ),
            name=name,
        )(*ins)

    early, edge23, total_a = call(
        own_kernel, "own", 9, 90,
        (feature, conv_weight, bias, down),
        [whole(feature.shape), *weights(lambda s: (2 - s // 3, (1 + 2 * (s % 3)) % 3))],
        [early_shape, edges, totals],
        [pltpu.VMEM((height, frames, channels, width), F32), pltpu.VMEM((height, frames, width, 3 * channels), BF16)],
    )
    edge01, total_b = call(
        earlier_kernel, "earlier", 6, 30,
        (flags, earlier, early, conv_weight, bias, down),
        [flag_spec, whole(earlier.shape), whole(early_shape.shape), *weights(lambda s: (s // 3, (1 + 2 * (s % 3)) % 3))],
        [edges, totals],
        [pltpu.VMEM((height, 2, channels, width), F32), pltpu.VMEM((height, 2, width, 3 * channels), BF16)],
    )
    up, dn, edge01, edge23 = lax.optimization_barrier((up, dn, edge01, edge23))
    corner = shifted(jnp.concatenate([up[2:], dn[2:]], axis=1), 1, 0)
    edge_scratch = [
        pltpu.VMEM((2, 2, channels, width), F32),
        pltpu.VMEM((2, 4, width, 3 * channels), BF16),
        pltpu.VMEM((2, lanes, width), F32),
        pltpu.VMEM((width, lanes), F32),
    ]
    edge_weights = weights(lambda s: (s // 2, 2 * (s % 2)))
    late, carry = call(
        late_edge_kernel, "late_edges", 6, 12,
        (flags, up, dn, edge23, total_a, conv_weight, bias, down),
        [flag_spec, whole(up.shape), whole(dn.shape), whole(edges.shape), whole(totals.shape), *edge_weights],
        [jax.ShapeDtypeStruct((lanes, width), F32), jax.ShapeDtypeStruct((quarter, 4 * z), F32)],
        edge_scratch,
    )
    carry = shifted(carry, 1, 0)
    halo_spec = whole((2, 1, width, channels))
    (out,) = call(
        early_edge_kernel, "early_edges", 6, 12,
        (flags, up, dn, corner, edge01, total_b, late, conv_weight, bias, down, patch_bias),
        [
            flag_spec, halo_spec, halo_spec, whole(corner.shape), whole(edges.shape), whole(totals.shape),
            whole(late.shape), *edge_weights, whole(patch_bias.shape),
        ],
        [jax.ShapeDtypeStruct((2, quarter, 4 * z), F32)],
        edge_scratch,
    )

    half = n_row // 2

    def routed(value, slot):
        pairs = []
        for t in range(n_tm):
            for r in range(n_row):
                target = r // 2 if (r % 2 == 0) == (slot == 0) else half + r // 2
                pairs.append((t * n_row + r, t * n_row + target))
        return lax.ppermute(value, AXES, pairs)

    first = out[0] + jnp.where(tm > 0, carry, 0.0)
    last = out[1]
    is_even = row % 2 == 0
    got_a = routed(jnp.where(is_even, first, last), 0)
    got_b = routed(jnp.where(is_even, last, first), 1)
    low = row < half
    return jnp.concatenate([jnp.where(low, got_a, got_b), jnp.where(low, got_b, got_a)], axis=0)


def solution(mesh):
    return jax.shard_map(
        on_device,
        mesh=mesh,
        in_specs=(P("tm", "row", None, None), P(), P(), P(), P()),
        out_specs=P(AXES, None),
        check_vma=False,
    )
```

```python
import jax
import jax.numpy as jnp
from jax import lax
from jax.experimental import pallas as pl
from jax.experimental.pallas import tpu as pltpu
from jax.sharding import PartitionSpec as P

F32 = jnp.float32
BF16 = jnp.bfloat16
VMEM_LIMIT = 28 * 1024 * 1024
AXES = ("tm", "row")


def widen(rows, target, keep=None):
    width, channels = rows.shape
    if keep is not None:
        rows = jnp.where(keep, rows.astype(F32), 0.0).astype(BF16)
    value = rows.astype(F32)
    column = lax.broadcasted_iota(jnp.int32, (width, channels), 0)
    before = jnp.where(column == 0, 0.0, pltpu.roll(value, 1, 0))
    after = jnp.where(column == width - 1, 0.0, pltpu.roll(value, width - 1, 0))
    target[:, 0:channels] = before.astype(BF16)
    target[:, channels : 2 * channels] = rows
    target[:, 2 * channels : 3 * channels] = after.astype(BF16)


def tap_product(weight, positions):
    channels = weight.shape[-1]
    weight = weight.reshape(3 * channels, channels)
    positions = positions.reshape(-1, 3 * channels)
    return lax.dot_general(weight, positions, (((0,), (1,)), ((), ())), preferred_element_type=F32)


def projected(pre, bias, down_ref, f, rows):
    taps = (1,) if f % 2 == 0 else (2, 0)
    act = []
    for value in pre:
        value = value + bias
        act.append((value / (1.0 + jnp.exp(-value))).astype(BF16))
    weight = []
    for a in taps:
        for i in rows:
            parts = [down_ref[a, i % 2, dx] for dx in (0, 0, 1, 1)]
            weight.append(jnp.concatenate(parts, axis=0))
    product = jnp.dot(jnp.concatenate(weight, axis=0), jnp.concatenate(act, axis=1), preferred_element_type=F32)
    width = pre[0].shape[1]
    size = weight[0].shape[0]
    found = {}
    for n, a in enumerate(taps):
        for half in range(2):
            first = (2 * n + half) * size
            found[a, half] = product[first : first + size, half * width : (half + 1) * width]
    return found


def add_products(found, a, total_ref):
    for half in range(2):
        value = found[a, half]
        size = value.shape[0] // 2
        for dx in range(2):
            first = dx * 2 * size + half * size
            total_ref[first : first + size, :] += value[dx * size : (dx + 1) * size]


def fold(total, d_ref):
    d_ref[...] = total.T
    lanes = total.shape[0]
    count = total.shape[1] // 4
    lane = lax.broadcasted_iota(jnp.int32, (count, lanes), 1)
    result = jnp.zeros((count, lanes), F32)
    for s in range(4):
        keep = (lane // (lanes // 2) == s % 2) & ((lane // (lanes // 8)) % 2 == s // 2)
        result = result + jnp.where(keep, d_ref[pl.ds(s, count, stride=4), :], 0.0)
    return (result + pltpu.roll(result, lanes // 2, 1))[:, : lanes // 2]


def bias_columns(bias_ref, width):
    return jnp.broadcast_to(bias_ref[...], (width, bias_ref.shape[1])).T


def copies(pairs, sems, first=0):
    started = []
    for n, (source, target) in enumerate(pairs):
        started.append(pltpu.make_async_copy(source, target, sems.at[first + n]))
        started[-1].start()
    return started


def tap_rows(tap_row, height):
    return range(max(0, tap_row - 1), min(height, height + tap_row - 1))


def send_kernel(x_ref, up_ref, dn_ref, late_ref, sems):
    height = x_ref.shape[1]
    pairs = [(x_ref.at[:, height - 1 :], up_ref), (x_ref.at[:, :1], dn_ref), (x_ref.at[2:], late_ref)]
    for copy in copies(pairs, sems):
        copy.wait()


def own_kernel(x_ref, w_ref, bias_ref, down_ref, acc, weights, total_ref, rows_in, wide, sems):
    frames, height, width, channels = x_ref.shape
    order = [(a, b) for a in (2, 1, 0) for b in (1, 0, 2)]
    fetch = copies([(x_ref, rows_in)] + [(w_ref.at[t], weights.at[t]) for t in order], sems)
    fetch[0].wait()

    def one(n, carry):
        f, h = n // height, n % height
        widen(rows_in[f, h], wide.at[h, f])
        return carry

    lax.fori_loop(0, frames * height, one, 0)
    for n, (tap_time, tap_row) in enumerate(order):
        fetch[1 + n].wait()
        count = frames - 2 + tap_time
        rows = tap_rows(tap_row, height)
        product = tap_product(weights[tap_time, tap_row], wide[rows[0] : rows[-1] + 1, :count])
        for m, h in enumerate(rows):
            for g in range(count):
                first = (m * count + g) * width
                value = product[:, first : first + width]
                target = (h + 1 - tap_row, g + 2 - tap_time)
                if n == 0:
                    acc[target] = value
                else:
                    acc[target] += value
    bias = bias_columns(bias_ref, width)
    total_ref[...] = jnp.zeros_like(total_ref)
    for f in (2, 3):
        found = projected([acc[1, f], acc[2, f]], bias, down_ref, f, (1, 2))
        add_products(found, 2 - (f + 1) % 2, total_ref.at[0])
        if f == 3:
            add_products(found, 0, total_ref.at[1])


def earlier_kernel(flag_ref, x_ref, acc_in, weights, bias_ref, down_ref, edge_ref, total_ref, acc, rows_in, wide, sems):
    frames, height, width, channels = x_ref.shape
    (fetch,) = copies([(x_ref, rows_in)], sems)
    fetch.wait()
    keep = flag_ref[2] == 1

    def one(n, carry):
        f, h = n // height, n % height
        widen(rows_in[f, h], wide.at[h, f], keep)
        return carry

    lax.fori_loop(0, frames * height, one, 0)
    for tap_time in (0, 1):
        for tap_row in (1, 0, 2):
            rows = tap_rows(tap_row, height)
            count = frames - tap_time
            product = tap_product(weights[tap_time, tap_row], wide[rows[0] : rows[-1] + 1, tap_time:])
            for m, h in enumerate(rows):
                for f in range(count):
                    first = (m * count + f) * width
                    value = product[:, first : first + width]
                    target = (h + 1 - tap_row, f)
                    if (tap_time, tap_row) == (0, 1):
                        acc[target] = acc_in[target] + value
                    else:
                        acc[target] += value
    for side, i in enumerate((0, height - 1)):
        for f in (0, 1):
            edge_ref[side, f] = acc[i, f]
    bias = bias_columns(bias_ref, width)
    total_ref[...] = jnp.zeros_like(total_ref)
    for f in (0, 1):
        found = projected([acc[1, f], acc[2, f]], bias, down_ref, f, (1, 2))
        add_products(found, 2 - (f + 1) % 2, total_ref.at[0])
        if f == 1:
            add_products(found, 0, total_ref.at[1])


def edge_taps(keep, initial, weights, bias_ref, down_ref, acc, rows_in, wide, total):
    width = wide.shape[2]
    for side in range(2):
        for n in range(4):
            widen(rows_in[side, n], wide.at[side, n], keep(side, n))
    for tap_time in range(3):
        for side in range(2):
            product = tap_product(weights[tap_time, 2 * side], wide[side, tap_time : tap_time + 2])
            for f in range(2):
                value = product[:, f * width : (f + 1) * width]
                if tap_time == 0:
                    acc[side, f] = initial(side, f) + value
                else:
                    acc[side, f] += value
    bias = bias_columns(bias_ref, width)
    for f in (0, 1):
        found = projected([acc[0, f], acc[1, f]], bias, down_ref, f, (0, 3))
        add_products(found, 2 - (f + 1) % 2, total.at[0])
        if f == 1:
            add_products(found, 0, total.at[1])


def late_edge_kernel(
    flag_ref, up, dn, acc_in, total_in, weights, bias_ref, down_ref, late_ref, carry_ref, acc, rows_in, wide, total, d_ref, sems
):
    for copy in copies([(up.at[:, 0], rows_in.at[0]), (dn.at[:, 0], rows_in.at[1])], sems):
        copy.wait()
    total[...] = total_in[...]
    edge_taps(
        lambda side, n: flag_ref[side] == 1, lambda side, f: acc_in[3 * side, f + 2], weights, bias_ref, down_ref, acc, rows_in,
        wide, total,
    )
    late_ref[...] = total[0]
    carry_ref[...] = fold(total[1], d_ref)


def early_edge_kernel(
    flag_ref, up, dn, corner, edge_in, total_in, late_in, weights, bias_ref, down_ref, down_bias_ref, out_ref, acc, rows_in, wide,
    total, d_ref, sems,
):
    pairs = []
    for side, ref in enumerate((up, dn)):
        pairs += [(corner.at[:, side], rows_in.at[side, :2]), (ref.at[:2, 0], rows_in.at[side, 2:])]
    for copy in copies(pairs, sems):
        copy.wait()
    total[...] = total_in[...]

    def keep(side, n):
        exists = flag_ref[side] == 1
        return exists & (flag_ref[2] == 1) if n < 2 else exists

    edge_taps(
        keep, lambda side, f: edge_in[side, f], weights, bias_ref, down_ref, acc, rows_in, wide, total
    )
    out_ref[0] = fold(total[0], d_ref) + down_bias_ref[...]
    out_ref[1] = fold(total[1] + late_in[...], d_ref) + down_bias_ref[...]


def on_device(feature, conv_weight, conv_bias, down_weight, down_bias):
    frames, height, width, channels = feature.shape
    z = down_bias.shape[0]
    n_tm, n_row = lax.axis_size("tm"), lax.axis_size("row")
    tm, row = lax.axis_index("tm"), lax.axis_index("row")
    quarter, lanes = width // 4, 8 * z

    def shifted(value, by_tm, by_row):
        pairs = [
            (t * n_row + r, (t + by_tm) % n_tm * n_row + (r + by_row) % n_row) for t in range(n_tm) for r in range(n_row)
        ]
        return lax.ppermute(value, AXES, pairs)

    any_ref, smem = pl.BlockSpec(memory_space=pl.ANY), pl.BlockSpec(memory_space=pltpu.SMEM)
    vmem = pl.BlockSpec(memory_space=pltpu.VMEM)

    def call(kernel, name, units, ins, specs, outs, scratch, copied):
        return pl.pallas_call(
            kernel,
            in_specs=specs,
            out_specs=[any_ref if isinstance(o, jax.ShapeDtypeStruct) else vmem for o in outs],
            out_shape=outs,
            scratch_shapes=[*scratch, pltpu.SemaphoreType.DMA((copied,))],
            compiler_params=pltpu.CompilerParams(vmem_limit_bytes=VMEM_LIMIT),
            cost_estimate=pl.CostEstimate(
                flops=units * width * 6 * channels * channels, bytes_accessed=4_000_000, transcendentals=0
            ),
            name=name,
        )(*ins)

    flags = jnp.stack([row > 0, row < n_row - 1, tm > 0]).astype(jnp.int32)
    edge_rows = jax.ShapeDtypeStruct((frames, 1, width, channels), BF16)
    up, dn, earlier = call(
        send_kernel, "send", 1, (feature,), [any_ref],
        [edge_rows, edge_rows, jax.ShapeDtypeStruct((2, height, width, channels), BF16)], [], 3,
    )
    up = shifted(up, 0, 1)
    dn = shifted(dn, 0, -1)
    earlier = shifted(earlier, 1, 0)

    bias = conv_bias.reshape(1, channels)
    down = down_weight.transpose(0, 1, 2, 4, 3)
    patch_bias = jnp.tile(down_bias, 4).reshape(1, 4 * z)
    totals = pltpu.VMEM((2, lanes, width), F32)
    edges = pltpu.VMEM((2, 2, channels, width), F32)

    acc, weights, total_a = call(
        own_kernel, "own", 90,
        (feature, conv_weight, bias, down), [any_ref, any_ref, vmem, vmem],
        [pltpu.VMEM((height, frames, channels, width), F32), pltpu.VMEM(conv_weight.shape, BF16), totals],
        [pltpu.VMEM(feature.shape, BF16), pltpu.VMEM((height, frames, width, 3 * channels), BF16)], 10,
    )
    edge01, total_b = call(
        earlier_kernel, "earlier", 30,
        (flags, earlier, acc, weights, bias, down), [smem, any_ref, vmem, vmem, vmem, vmem],
        [edges, totals],
        [
            pltpu.VMEM((height, 2, channels, width), F32), pltpu.VMEM(earlier.shape, BF16),
            pltpu.VMEM((height, 2, width, 3 * channels), BF16),
        ], 1,
    )
    up, dn, edge01, acc = lax.optimization_barrier((up, dn, edge01, acc))
    corner = shifted(jnp.concatenate([up[2:], dn[2:]], axis=1), 1, 0)
    edge_scratch = [
        pltpu.VMEM((2, 2, channels, width), F32),
        pltpu.VMEM((2, 4, width, channels), BF16),
        pltpu.VMEM((2, 4, width, 3 * channels), BF16),
        pltpu.VMEM((2, lanes, width), F32),
        pltpu.VMEM((width, lanes), F32),
    ]
    late, carry = call(
        late_edge_kernel, "late_edges", 12,
        (flags, up, dn, acc, total_a, weights, bias, down), [smem, any_ref, any_ref, vmem, vmem, vmem, vmem, vmem],
        [pltpu.VMEM((lanes, width), F32), pltpu.VMEM((quarter, 4 * z), F32)], edge_scratch, 2,
    )
    carry = shifted(carry, 1, 0)
    (out,) = call(
        early_edge_kernel, "early_edges", 12,
        (flags, up, dn, corner, edge01, total_b, late, weights, bias, down, patch_bias),
        [smem, any_ref, any_ref, any_ref, vmem, vmem, vmem, vmem, vmem, vmem, vmem],
        [pltpu.VMEM((2, quarter, 4 * z), F32)], edge_scratch, 4,
    )

    half = n_row // 2

    def routed(value, slot):
        pairs = []
        for t in range(n_tm):
            for r in range(n_row):
                target = r // 2 if (r % 2 == 0) == (slot == 0) else half + r // 2
                pairs.append((t * n_row + r, t * n_row + target))
        return lax.ppermute(value, AXES, pairs)

    first = out[0] + jnp.where(tm > 0, carry, 0.0)
    last = out[1]
    is_even = row % 2 == 0
    got_a = routed(jnp.where(is_even, first, last), 0)
    got_b = routed(jnp.where(is_even, last, first), 1)
    low = row < half
    return jnp.concatenate([jnp.where(low, got_a, got_b), jnp.where(low, got_b, got_a)], axis=0)


def solution(mesh):
    return jax.shard_map(
        on_device,
        mesh=mesh,
        in_specs=(P("tm", "row", None, None), P(), P(), P(), P()),
        out_specs=P(AXES, None),
        check_vma=False,
    )
```

```python
import jax
import jax.numpy as jnp
from jax import lax
from jax.experimental import pallas as pl
from jax.experimental.pallas import tpu as pltpu
from jax.sharding import PartitionSpec as P

F32 = jnp.float32
BF16 = jnp.bfloat16
VMEM_LIMIT = 20 * 1024 * 1024
AXES = ("tm", "row")
HALO = pl.ANY


def widen(rows, target, keep=None):
    width, channels = rows.shape
    if keep is not None:
        rows = jnp.where(keep, rows.astype(F32), 0.0).astype(BF16)
    value = rows.astype(F32)
    column = lax.broadcasted_iota(jnp.int32, (width, channels), 0)
    before = jnp.where(column == 0, 0.0, pltpu.roll(value, 1, 0))
    after = jnp.where(column == width - 1, 0.0, pltpu.roll(value, width - 1, 0))
    target[:, 0:channels] = before.astype(BF16)
    target[:, channels : 2 * channels] = rows
    target[:, 2 * channels : 3 * channels] = after.astype(BF16)


def tap_product(weight, positions):
    channels = weight.shape[-1]
    weight = weight.reshape(3 * channels, channels)
    positions = positions.reshape(-1, 3 * channels)
    return lax.dot_general(weight, positions, (((0,), (1,)), ((), ())), preferred_element_type=F32)


def projected(pre, bias, down_ref, f, rows):
    taps = (1,) if f % 2 == 0 else (2, 0)
    act = []
    for value in pre:
        value = value + bias
        act.append((value / (1.0 + jnp.exp(-value))).astype(BF16))
    weight = []
    for a in taps:
        for i in rows:
            parts = [down_ref[a, i % 2, dx] for dx in (0, 0, 1, 1)]
            weight.append(jnp.concatenate(parts, axis=0))
    product = jnp.dot(jnp.concatenate(weight, axis=0), jnp.concatenate(act, axis=1), preferred_element_type=F32)
    width = pre[0].shape[1]
    size = weight[0].shape[0]
    found = {}
    for n, a in enumerate(taps):
        for half in range(2):
            first = (2 * n + half) * size
            found[a, half] = product[first : first + size, half * width : (half + 1) * width]
    return found


def add_products(found, a, total_ref):
    for half in range(2):
        value = found[a, half]
        size = value.shape[0] // 2
        for dx in range(2):
            first = dx * 2 * size + half * size
            total_ref[first : first + size, :] += value[dx * size : (dx + 1) * size]


def fold(total, d_ref):
    d_ref[...] = total.T
    lanes = total.shape[0]
    count = total.shape[1] // 4
    lane = lax.broadcasted_iota(jnp.int32, (count, lanes), 1)
    result = jnp.zeros((count, lanes), F32)
    for s in range(4):
        keep = (lane // (lanes // 2) == s % 2) & ((lane // (lanes // 8)) % 2 == s // 2)
        result = result + jnp.where(keep, d_ref[pl.ds(s, count, stride=4), :], 0.0)
    return (result + pltpu.roll(result, lanes // 2, 1))[:, : lanes // 2]


def exists(side):
    if side == 2:
        return lax.axis_index("tm") > 0
    row = lax.axis_index("row")
    return row > 0 if side == 0 else row < lax.axis_size("row") - 1


def copies(pairs, sems, first=0):
    started = []
    for n, (source, target) in enumerate(pairs):
        started.append(pltpu.make_async_copy(source, target, sems.at[first + n]))
        started[-1].start()
    return started


def tap_rows(tap_row, height):
    return range(max(0, tap_row - 1), min(height, height + tap_row - 1))


def send_kernel(x_ref, up_ref, dn_ref, late_ref, sems):
    height = x_ref.shape[1]
    pairs = [(x_ref.at[:, height - 1 :], up_ref), (x_ref.at[:, :1], dn_ref), (x_ref.at[2:], late_ref)]
    for copy in copies(pairs, sems):
        copy.wait()


def relay_kernel(up, dn, out_ref, sems):
    for copy in copies([(up.at[2:], out_ref.at[:, :1]), (dn.at[2:], out_ref.at[:, 1:])], sems):
        copy.wait()


def own_kernel(x_ref, w_ref, bias_in, down_in, acc, weights, bias_ref, down_ref, totals, rows_in, bias_row, wide, sems):
    frames, height, width, channels = x_ref.shape
    order = [(a, b) for a in (2, 1, 0) for b in (1, 0, 2)]
    fetch = copies(
        [(x_ref, rows_in)] + [(w_ref.at[t], weights.at[t]) for t in order] + [(bias_in, bias_row), (down_in, down_ref)], sems
    )
    fetch[0].wait()

    def one(n, carry):
        f, h = n // height, n % height
        widen(rows_in[f, h], wide.at[h, f])
        return carry

    lax.fori_loop(0, frames * height, one, 0)
    for n, (tap_time, tap_row) in enumerate(order):
        fetch[1 + n].wait()
        count = frames - 2 + tap_time
        rows = tap_rows(tap_row, height)
        product = tap_product(weights[tap_time, tap_row], wide[rows[0] : rows[-1] + 1, :count])
        for m, h in enumerate(rows):
            for g in range(count):
                first = (m * count + g) * width
                value = product[:, first : first + width]
                target = (h + 1 - tap_row, g + 2 - tap_time)
                if n == 0:
                    acc[target] = value
                else:
                    acc[target] += value
    fetch[-2].wait()
    fetch[-1].wait()
    bias_ref[...] = jnp.broadcast_to(bias_row[...].reshape(1, channels), (width, channels)).T
    totals[...] = jnp.zeros_like(totals)
    project_rows(acc, (2, 3), (1, 2), bias_ref, down_ref, totals)


def project_rows(acc, frames, rows, bias_ref, down_ref, totals):
    for f in frames:
        found = projected([acc[i, f] for i in rows], bias_ref[...], down_ref, f, rows)
        add_products(found, 1 + f % 2, totals.at[f // 2])
        if f % 2 == 1:
            add_products(found, 0, totals.at[f // 2 + 1])


def earlier_kernel(x_ref, acc_in, weights, bias_ref, down_ref, totals_in, edge_ref, totals_ref, rows_in, acc, totals, wide, sems):
    frames, height, width, channels = x_ref.shape
    (fetch,) = copies([(x_ref, rows_in)], sems)
    moved = copies([(acc_in.at[side * (height - 1), 2:], edge_ref.at[side, 2:]) for side in range(2)], sems, 1)
    totals[...] = totals_in[...]
    keep = exists(2)
    fetch.wait()

    def one(n, carry):
        f, h = n // height, n % height
        widen(rows_in[f, h], wide.at[h, f], keep)
        return carry

    lax.fori_loop(0, frames * height, one, 0)
    for tap_time in (0, 1):
        for tap_row in (1, 0, 2):
            rows = tap_rows(tap_row, height)
            count = frames - tap_time
            product = tap_product(weights[tap_time, tap_row], wide[rows[0] : rows[-1] + 1, tap_time:])
            for m, h in enumerate(rows):
                for f in range(count):
                    first = (m * count + f) * width
                    target = (h + 1 - tap_row, f)
                    value = acc_in[target] if (tap_time, tap_row) == (0, 1) else acc[target]
                    acc[target] = value + product[:, first : first + width]
    moved += copies([(acc.at[side * (height - 1)], edge_ref.at[side, :2]) for side in range(2)], sems, 3)
    project_rows(acc, (0, 1), (1, 2), bias_ref, down_ref, totals)
    moved += copies([(totals, totals_ref)], sems, 5)
    for copy in moved:
        copy.wait()


def edge_taps(pairs, keep, first, edge_ref, totals_in, w_ref, bias_in, down_in, scratch):
    acc, rows_in, weights, wide, bias_row, down_ref, totals, d_ref, sems = scratch
    width, channels = rows_in.shape[2:]
    taps = [(a, side) for a in range(3) for side in range(2)]
    brought = copies(pairs, sems)
    heavy = copies([(w_ref.at[a, 2 * side], weights.at[n]) for n, (a, side) in enumerate(taps)], sems, 4)
    rest = copies(
        [(edge_ref.at[:, first : first + 2], acc), (totals_in, totals), (bias_in, bias_row), (down_in, down_ref)], sems, 10
    )
    for copy in brought:
        copy.wait()
    for side in range(2):
        for n in range(4):
            widen(rows_in[side, n], wide.at[side, n], keep(side, n))
    rest[0].wait()
    for n, (tap_time, side) in enumerate(taps):
        heavy[n].wait()
        product = tap_product(weights[n], wide[side, tap_time : tap_time + 2])
        for f in range(2):
            acc[side, f] += product[:, f * width : (f + 1) * width]
    for copy in rest[1:]:
        copy.wait()
    bias = jnp.broadcast_to(bias_row[...].reshape(1, channels), (width, channels)).T
    for f in (first, first + 1):
        found = projected([acc[side, f - first] for side in range(2)], bias, down_ref, f, (0, 3))
        add_products(found, 1 + f % 2, totals.at[f // 2])
        if f % 2 == 1:
            add_products(found, 0, totals.at[f // 2 + 1])


def late_edge_kernel(up, dn, edge_ref, totals_in, w_ref, bias_in, down_in, totals_ref, carry_ref, *scratch):
    pairs = [(ref.at[:, 0], scratch[1].at[side]) for side, ref in enumerate((up, dn))]
    edge_taps(pairs, lambda side, n: exists(side), 2, edge_ref, totals_in, w_ref, bias_in, down_in, scratch)
    totals, d_ref, sems = scratch[-3:]
    (moved,) = copies([(totals, totals_ref)], sems)
    carry_ref[...] = fold(totals[2], d_ref)
    moved.wait()


def early_edge_kernel(up, dn, corner, edge_ref, totals_in, w_ref, bias_in, down_in, down_bias_ref, out_ref, *scratch):
    pairs = []
    for side, ref in enumerate((up, dn)):
        pairs += [(corner.at[:, side], scratch[1].at[side, :2]), (ref.at[:2, 0], scratch[1].at[side, 2:])]
    edge_taps(
        pairs, lambda side, n: exists(side) & exists(2) if n < 2 else exists(side), 0, edge_ref, totals_in, w_ref, bias_in,
        down_in, scratch,
    )
    totals, d_ref = scratch[-3:-1]
    latent_bias = down_bias_ref[...].reshape(1, -1)
    latent_bias = jnp.concatenate([latent_bias] * 4, axis=1)
    for t in range(2):
        out_ref[t] = fold(totals[t], d_ref) + latent_bias


def on_device(feature, conv_weight, conv_bias, down_weight, down_bias):
    frames, height, width, channels = feature.shape
    z = down_bias.shape[0]
    n_tm, n_row = lax.axis_size("tm"), lax.axis_size("row")
    tm, row = lax.axis_index("tm"), lax.axis_index("row")
    quarter, lanes = width // 4, 8 * z

    def shifted(value, by_tm, by_row):
        pairs = [
            (t * n_row + r, (t + by_tm) % n_tm * n_row + (r + by_row) % n_row) for t in range(n_tm) for r in range(n_row)
        ]
        return lax.ppermute(value, AXES, pairs)

    hbm_ref, halo_ref = pl.BlockSpec(memory_space=pltpu.HBM), pl.BlockSpec(memory_space=HALO)
    vmem = pl.BlockSpec(memory_space=pltpu.VMEM)

    def in_hbm(value):
        return pltpu.with_memory_space_constraint(value, pltpu.HBM)

    def call(kernel, name, units, ins, specs, outs, out_specs, scratch, copied):
        return pl.pallas_call(
            kernel,
            in_specs=specs,
            out_specs=out_specs,
            out_shape=outs,
            scratch_shapes=[*scratch, pltpu.SemaphoreType.DMA((copied,))],
            compiler_params=pltpu.CompilerParams(vmem_limit_bytes=VMEM_LIMIT),
            cost_estimate=pl.CostEstimate(
                flops=units * width * 6 * channels * channels, bytes_accessed=4_000_000, transcendentals=0
            ),
            name=name,
        )(*[in_hbm(i) if spec is hbm_ref else i for i, spec in zip(ins, specs)])

    up, dn, earlier = call(
        send_kernel, "send", 1, (feature,), [hbm_ref],
        [
            pltpu.HBM((frames, 1, width, channels), BF16), pltpu.HBM((frames, 1, width, channels), BF16),
            pltpu.HBM((2, height, width, channels), BF16),
        ],
        [hbm_ref] * 3, [], 3,
    )
    up = shifted(up, 0, 1)
    dn = shifted(dn, 0, -1)
    earlier = shifted(earlier, 1, 0)

    down = down_weight.transpose(0, 1, 2, 4, 3)
    totals_shape = (3, lanes, width)
    kept = call(
        own_kernel, "own", 90, (feature, conv_weight, conv_bias, down), [hbm_ref] * 4,
        [
            pltpu.VMEM((height, frames, channels, width), F32), pltpu.VMEM(conv_weight.shape, BF16),
            pltpu.VMEM((channels, width), F32), pltpu.VMEM(down.shape, BF16), pltpu.VMEM(totals_shape, F32),
        ],
        [vmem] * 5,
        [
            pltpu.VMEM(feature.shape, BF16), pltpu.VMEM(conv_bias.shape, F32),
            pltpu.VMEM((height, frames, width, 3 * channels), BF16),
        ], 12,
    )
    edges, totals = call(
        earlier_kernel, "earlier", 30, (earlier, *kept), [halo_ref] + [vmem] * 5,
        [pltpu.HBM((2, frames, channels, width), F32), pltpu.HBM(totals_shape, F32)], [hbm_ref] * 2,
        [
            pltpu.VMEM(earlier.shape, BF16), pltpu.VMEM((height, 2, channels, width), F32), pltpu.VMEM(totals_shape, F32),
            pltpu.VMEM((height, 2, width, 3 * channels), BF16),
        ], 6,
    )
    up, dn, totals = lax.optimization_barrier((up, dn, totals))
    (corner,) = call(
        relay_kernel, "relay", 1, (up, dn), [halo_ref, halo_ref],
        [pltpu.HBM((2, 2, width, channels), BF16)], [hbm_ref], [], 2,
    )
    corner = shifted(corner, 1, 0)
    edge_scratch = [
        pltpu.VMEM((2, 2, channels, width), F32), pltpu.VMEM((2, 4, width, channels), BF16),
        pltpu.VMEM((6, 3, channels, channels), BF16), pltpu.VMEM((2, 4, width, 3 * channels), BF16),
        pltpu.VMEM(conv_bias.shape, F32), pltpu.VMEM(down.shape, BF16), pltpu.VMEM(totals_shape, F32),
        pltpu.VMEM((width, lanes), F32),
    ]
    totals, carry = call(
        late_edge_kernel, "late_edges", 12, (up, dn, edges, totals, conv_weight, conv_bias, down),
        [halo_ref, halo_ref] + [hbm_ref] * 5,
        [pltpu.HBM(totals_shape, F32), jax.ShapeDtypeStruct((quarter, 4 * z), F32)], [hbm_ref, vmem], edge_scratch, 14,
    )
    carry = shifted(carry, 1, 0)
    (out,) = call(
        early_edge_kernel, "early_edges", 12, (up, dn, corner, edges, totals, conv_weight, conv_bias, down, down_bias),
        [halo_ref] * 3 + [hbm_ref] * 5 + [vmem],
        [jax.ShapeDtypeStruct((2, quarter, 4 * z), F32)], [vmem], edge_scratch, 14,
    )

    half = n_row // 2

    def routed(value, slot):
        pairs = []
        for t in range(n_tm):
            for r in range(n_row):
                target = r // 2 if (r % 2 == 0) == (slot == 0) else half + r // 2
                pairs.append((t * n_row + r, t * n_row + target))
        return lax.ppermute(value, AXES, pairs)

    first = out[0] + jnp.where(tm > 0, carry, 0.0)
    last = out[1]
    is_even = row % 2 == 0
    got_a = routed(jnp.where(is_even, first, last), 0)
    got_b = routed(jnp.where(is_even, last, first), 1)
    low = row < half
    return jnp.concatenate([jnp.where(low, got_a, got_b), jnp.where(low, got_b, got_a)], axis=0)


def solution(mesh):
    return jax.shard_map(
        on_device,
        mesh=mesh,
        in_specs=(P("tm", "row", None, None), P(), P(), P(), P()),
        out_specs=P(AXES, None),
        check_vma=False,
    )
```

```python
import jax
import jax.numpy as jnp
from jax import lax
from jax.experimental import pallas as pl
from jax.experimental.pallas import tpu as pltpu
from jax.sharding import PartitionSpec as P

F32 = jnp.float32
BF16 = jnp.bfloat16
VMEM_LIMIT = 24 * 1024 * 1024
AXES = ("tm", "row")
HALO = pl.ANY


def widen(rows, target, keep=None):
    width, channels = rows.shape
    if keep is not None:
        rows = jnp.where(keep, rows.astype(F32), 0.0).astype(BF16)
    value = rows.astype(F32)
    column = lax.broadcasted_iota(jnp.int32, (width, channels), 0)
    before = jnp.where(column == 0, 0.0, pltpu.roll(value, 1, 0))
    after = jnp.where(column == width - 1, 0.0, pltpu.roll(value, width - 1, 0))
    target[:, 0:channels] = before.astype(BF16)
    target[:, channels : 2 * channels] = rows
    target[:, 2 * channels : 3 * channels] = after.astype(BF16)


def tap_product(weight, positions):
    positions = positions.reshape(-1, weight.shape[1])
    return lax.dot_general(weight, positions, (((1,), (1,)), ((), ())), preferred_element_type=F32)


def projected(pre, bias, down_ref, f, rows):
    taps = (1,) if f % 2 == 0 else (2, 0)
    act = []
    for value in pre:
        value = value + bias
        act.append((value / (1.0 + jnp.exp(-value))).astype(BF16))
    weight = []
    for a in taps:
        for i in rows:
            parts = [down_ref[a, i % 2, dx] for dx in (0, 0, 1, 1)]
            weight.append(jnp.concatenate(parts, axis=0))
    product = jnp.dot(jnp.concatenate(weight, axis=0), jnp.concatenate(act, axis=1), preferred_element_type=F32)
    width = pre[0].shape[1]
    size = weight[0].shape[0]
    found = {}
    for n, a in enumerate(taps):
        for half in range(2):
            first = (2 * n + half) * size
            found[a, half] = product[first : first + size, half * width : (half + 1) * width]
    return found


def add_products(found, a, total_ref):
    for half in range(2):
        value = found[a, half]
        size = value.shape[0] // 2
        for dx in range(2):
            first = dx * 2 * size + half * size
            total_ref[first : first + size, :] += value[dx * size : (dx + 1) * size]


def fold(total, d_ref):
    d_ref[...] = total.T
    lanes = total.shape[0]
    count = total.shape[1] // 4
    lane = lax.broadcasted_iota(jnp.int32, (count, lanes), 1)
    result = jnp.zeros((count, lanes), F32)
    for s in range(4):
        keep = (lane // (lanes // 2) == s % 2) & ((lane // (lanes // 8)) % 2 == s // 2)
        result = result + jnp.where(keep, d_ref[pl.ds(s, count, stride=4), :], 0.0)
    return (result + pltpu.roll(result, lanes // 2, 1))[:, : lanes // 2]


def exists(side):
    if side == 2:
        return lax.axis_index("tm") > 0
    row = lax.axis_index("row")
    return row > 0 if side == 0 else row < lax.axis_size("row") - 1


def copies(pairs, sems, first=0):
    started = []
    for n, (source, target) in enumerate(pairs):
        started.append(pltpu.make_async_copy(source, target, sems.at[first + n]))
        started[-1].start()
    return started


def tap_rows(tap_row, height):
    return range(max(0, tap_row - 1), min(height, height + tap_row - 1))


def send_kernel(x_ref, up_ref, dn_ref, late_ref, sems):
    height = x_ref.shape[1]
    pairs = [(x_ref.at[:, height - 1 :], up_ref), (x_ref.at[:, :1], dn_ref), (x_ref.at[2:], late_ref)]
    for copy in copies(pairs, sems):
        copy.wait()


def relay_kernel(up, dn, out_ref, sems):
    for copy in copies([(up.at[2:], out_ref.at[:, :1]), (dn.at[2:], out_ref.at[:, 1:])], sems):
        copy.wait()


def own_kernel(
    x_ref, w_ref, bias_in, down_in, acc, weights, bias_ref, down_ref, totals, edge_weights, rows_in, staged, bias_row, wide, sems
):
    frames, height, width, channels = x_ref.shape
    order = [(a, b) for a in (2, 1, 0) for b in (1, 0, 2)]
    heavy = copies([(w_ref.at[order[0]], staged.at[order[0]])], sems, frames)
    fetch = copies([(x_ref.at[f], rows_in.at[f]) for f in range(frames)], sems)
    small = copies([(bias_in, bias_row), (down_in, down_ref)], sems, frames + 9)
    heavy += copies([(w_ref.at[order[1]], staged.at[order[1]])], sems, frames + 1)
    moved = []
    for n, (tap_time, tap_row) in enumerate(order):
        heavy[n].wait()
        if n + 2 < len(order):
            heavy += copies([(w_ref.at[order[n + 2]], staged.at[order[n + 2]])], sems, frames + n + 2)
        weights[tap_time, tap_row] = staged[tap_time, tap_row].reshape(3 * channels, channels).T
        if tap_row != 1:
            moved += copies(
                [(weights.at[tap_time, tap_row], edge_weights.at[tap_time, tap_row // 2])], sems, frames + 11 + len(moved)
            )
        if n == 0:
            for f in range(frames):
                fetch[f].wait()
                for h in range(height):
                    widen(rows_in[f, h], wide.at[h, f])
                product = tap_product(weights[tap_time, tap_row], wide[:, f])
                for h in range(height):
                    acc[h, f] = product[:, h * width : (h + 1) * width]
            continue
        count = frames - 2 + tap_time
        rows = tap_rows(tap_row, height)
        product = tap_product(weights[tap_time, tap_row], wide[rows[0] : rows[-1] + 1, :count])
        for m, h in enumerate(rows):
            for g in range(count):
                first = (m * count + g) * width
                acc[h + 1 - tap_row, g + 2 - tap_time] += product[:, first : first + width]
    for copy in small:
        copy.wait()
    bias_ref[...] = jnp.broadcast_to(bias_row[...].reshape(1, channels), (width, channels)).T
    totals[...] = jnp.zeros_like(totals)
    for f in (2, 3):
        project_rows([acc[i, f] for i in (1, 2)], f, (1, 2), bias_ref[...], down_ref, totals)
    for copy in moved:
        copy.wait()


def project_rows(pre, f, rows, bias, down_ref, totals):
    found = projected(pre, bias, down_ref, f, rows)
    add_products(found, 1 + f % 2, totals.at[f // 2])
    if f % 2 == 1:
        add_products(found, 0, totals.at[f // 2 + 1])


def earlier_kernel(x_ref, acc_in, weights, bias_ref, down_ref, totals_in, edge_ref, totals_ref, rows_in, acc, totals, wide, sems):
    frames, height, width, channels = x_ref.shape
    (fetch,) = copies([(x_ref, rows_in)], sems)
    moved = copies([(acc_in.at[side * (height - 1), 2:], edge_ref.at[side, 2:]) for side in range(2)], sems, 1)
    totals[...] = totals_in[...]
    keep = exists(2)
    fetch.wait()

    def one(n, carry):
        f, h = n // height, n % height
        widen(rows_in[f, h], wide.at[h, f], keep)
        return carry

    lax.fori_loop(0, frames * height, one, 0)
    for tap_time in (0, 1):
        for tap_row in (1, 0, 2):
            rows = tap_rows(tap_row, height)
            count = frames - tap_time
            product = tap_product(weights[tap_time, tap_row], wide[rows[0] : rows[-1] + 1, tap_time:])
            for m, h in enumerate(rows):
                for f in range(count):
                    first = (m * count + f) * width
                    target = (h + 1 - tap_row, f)
                    value = acc_in[target] if (tap_time, tap_row) == (0, 1) else acc[target]
                    acc[target] = value + product[:, first : first + width]
    moved += copies([(acc.at[side * (height - 1)], edge_ref.at[side, :2]) for side in range(2)], sems, 3)
    for f in (0, 1):
        project_rows([acc[i, f] for i in (1, 2)], f, (1, 2), bias_ref[...], down_ref, totals)
    moved += copies([(totals, totals_ref)], sems, 5)
    for copy in moved:
        copy.wait()


def rows_kernel(
    up, dn, edge_in, w_ref, totals_in, bias_in, down_in, edge_ref, totals_ref, carry_ref,
    edge, weights, bias_row, down_ref, totals, sides_in, sides, d_ref, sems,
):
    width, channels = sides_in.shape[2:]
    order = [(a, side) for a in (2, 1, 0) for side in range(2)]
    brought = copies([(ref.at[:, 0], sides_in.at[side]) for side, ref in enumerate((up, dn))], sems, 6)
    heavy = copies([(w_ref.at[t], weights.at[n]) for n, t in enumerate(order[:2])], sems)
    initial = copies([(edge_in.at[side], edge.at[side]) for side in range(2)], sems, 8)
    heavy += copies([(w_ref.at[t], weights.at[n + 2]) for n, t in enumerate(order[2:])], sems, 2)
    late = copies([(totals_in, totals), (bias_in, bias_row), (down_in, down_ref)], sems, 10)
    for n, (tap_time, side) in enumerate(order):
        count = tap_time + 2
        if n < 2:
            brought[side].wait()
            for f in range(4):
                widen(sides_in[side, f], sides.at[side, f], exists(side))
        heavy[n].wait()
        product = tap_product(weights[n], sides[side, :count])
        if n < 2:
            initial[side].wait()
        for m in range(count):
            edge[side, m + 2 - tap_time] += product[:, m * width : (m + 1) * width]
    moved = copies([(edge.at[side, :2], edge_ref.at[side]) for side in range(2)], sems)
    for copy in late:
        copy.wait()
    bias = jnp.broadcast_to(bias_row[...].reshape(1, channels), (width, channels)).T
    for f in (2, 3):
        project_rows([edge[side, f] for side in range(2)], f, (0, 3), bias, down_ref, totals)
    moved += copies([(totals, totals_ref)], sems, 2)
    carry_ref[...] = fold(totals[2], d_ref)
    for copy in moved:
        copy.wait()


def corner_kernel(
    corner, edge_in, w_ref, totals_in, bias_in, down_in, down_bias_ref, out_ref,
    edge, weights, bias_row, down_ref, totals, sides_in, sides, d_ref, sems,
):
    width, channels = sides_in.shape[2:]
    order = [(a, side) for a in range(2) for side in range(2)]
    brought = copies([(corner.at[:, side], sides_in.at[side]) for side in range(2)], sems)
    heavy = copies([(w_ref.at[a, side], weights.at[a, side]) for a, side in order], sems, 2)
    rest = copies([(edge_in, edge), (totals_in, totals), (bias_in, bias_row), (down_in, down_ref)], sems, 6)
    for copy in brought:
        copy.wait()
    for side in range(2):
        for n in range(2):
            widen(sides_in[side, n], sides.at[side, n], exists(side) & exists(2))
    for n, (tap_time, side) in enumerate(order):
        heavy[n].wait()
        product = tap_product(weights[tap_time, side], sides[side, tap_time:])
        if n == 0:
            rest[0].wait()
        for f in range(2 - tap_time):
            edge[side, f] += product[:, f * width : (f + 1) * width]
    for copy in rest[1:]:
        copy.wait()
    bias = jnp.broadcast_to(bias_row[...].reshape(1, channels), (width, channels)).T
    for f in (0, 1):
        project_rows([edge[side, f] for side in range(2)], f, (0, 3), bias, down_ref, totals)
    latent_bias = down_bias_ref[...].reshape(1, -1)
    latent_bias = jnp.concatenate([latent_bias] * 4, axis=1)
    for t in range(2):
        out_ref[t] = fold(totals[t], d_ref) + latent_bias


def on_device(feature, conv_weight, conv_bias, down_weight, down_bias):
    frames, height, width, channels = feature.shape
    z = down_bias.shape[0]
    n_tm, n_row = lax.axis_size("tm"), lax.axis_size("row")
    tm, row = lax.axis_index("tm"), lax.axis_index("row")
    quarter, lanes = width // 4, 8 * z

    def shifted(value, by_tm, by_row):
        pairs = [
            (t * n_row + r, (t + by_tm) % n_tm * n_row + (r + by_row) % n_row) for t in range(n_tm) for r in range(n_row)
        ]
        return lax.ppermute(value, AXES, pairs)

    hbm_ref, halo_ref = pl.BlockSpec(memory_space=pltpu.HBM), pl.BlockSpec(memory_space=HALO)
    vmem = pl.BlockSpec(memory_space=pltpu.VMEM)

    def in_hbm(value):
        return pltpu.with_memory_space_constraint(value, pltpu.HBM)

    def call(kernel, name, units, ins, specs, outs, out_specs, scratch, copied):
        return pl.pallas_call(
            kernel,
            in_specs=specs,
            out_specs=out_specs,
            out_shape=outs,
            scratch_shapes=[*scratch, pltpu.SemaphoreType.DMA((copied,))],
            compiler_params=pltpu.CompilerParams(vmem_limit_bytes=VMEM_LIMIT),
            cost_estimate=pl.CostEstimate(
                flops=units * width * 6 * channels * channels, bytes_accessed=4_000_000, transcendentals=0
            ),
            name=name,
        )(*[in_hbm(i) if spec is hbm_ref else i for i, spec in zip(ins, specs)])

    up, dn, earlier = call(
        send_kernel, "send", 1, (feature,), [hbm_ref],
        [
            pltpu.VMEM((frames, 1, width, channels), BF16), pltpu.VMEM((frames, 1, width, channels), BF16),
            pltpu.VMEM((2, height, width, channels), BF16),
        ],
        [vmem] * 3, [], 3,
    )
    up = shifted(up, 0, 1)
    dn = shifted(dn, 0, -1)
    earlier = shifted(earlier, 1, 0)

    down = down_weight.transpose(0, 1, 2, 4, 3)
    totals_shape = (3, lanes, width)
    *kept, edge_weights = call(
        own_kernel, "own", 90, (feature, conv_weight, conv_bias, down), [hbm_ref] * 4,
        [
            pltpu.VMEM((height, frames, channels, width), F32), pltpu.VMEM((3, 3, channels, 3 * channels), BF16),
            pltpu.VMEM((channels, width), F32), pltpu.VMEM(down.shape, BF16), pltpu.VMEM(totals_shape, F32),
            pltpu.HBM((3, 2, channels, 3 * channels), BF16),
        ],
        [vmem] * 5 + [hbm_ref],
        [
            pltpu.VMEM(feature.shape, BF16), pltpu.VMEM(conv_weight.shape, BF16), pltpu.VMEM(conv_bias.shape, F32),
            pltpu.VMEM((height, frames, width, 3 * channels), BF16),
        ], frames + 17,
    )
    edges, totals = call(
        earlier_kernel, "earlier", 30, (earlier, *kept), [halo_ref] + [vmem] * 5,
        [pltpu.HBM((2, frames, channels, width), F32), pltpu.HBM(totals_shape, F32)], [hbm_ref] * 2,
        [
            pltpu.VMEM(earlier.shape, BF16), pltpu.VMEM((height, 2, channels, width), F32), pltpu.VMEM(totals_shape, F32),
            pltpu.VMEM((height, 2, width, 3 * channels), BF16),
        ], 6,
    )
    up, dn, totals = lax.optimization_barrier((up, dn, totals))
    (corner,) = call(
        relay_kernel, "relay", 1, (up, dn), [halo_ref, halo_ref],
        [pltpu.HBM((2, 2, width, channels), BF16)], [hbm_ref], [], 2,
    )
    corner = shifted(corner, 1, 0)
    edge_shape = (2, 2, channels, width)
    small = [pltpu.VMEM(conv_bias.shape, F32), pltpu.VMEM(down.shape, BF16), pltpu.VMEM(totals_shape, F32)]
    fold_space = pltpu.VMEM((width, lanes), F32)
    edges, totals, carry = call(
        rows_kernel, "rows", 18, (up, dn, edges, edge_weights, totals, conv_bias, down), [halo_ref] * 2 + [hbm_ref] * 5,
        [pltpu.HBM(edge_shape, F32), pltpu.HBM(totals_shape, F32), jax.ShapeDtypeStruct((quarter, 4 * z), F32)],
        [hbm_ref, hbm_ref, vmem],
        [
            pltpu.VMEM((2, frames, channels, width), F32), pltpu.VMEM((6, channels, 3 * channels), BF16), *small,
            pltpu.VMEM((2, frames, width, channels), BF16), pltpu.VMEM((2, frames, width, 3 * channels), BF16), fold_space,
        ], 13,
    )
    carry = shifted(carry, 1, 0)
    (out,) = call(
        corner_kernel, "corners", 6, (corner, edges, edge_weights, totals, conv_bias, down, down_bias),
        [halo_ref] + [hbm_ref] * 5 + [vmem],
        [jax.ShapeDtypeStruct((2, quarter, 4 * z), F32)], [vmem],
        [
            pltpu.VMEM(edge_shape, F32), pltpu.VMEM((2, 2, channels, 3 * channels), BF16), *small,
            pltpu.VMEM((2, 2, width, channels), BF16), pltpu.VMEM((2, 2, width, 3 * channels), BF16), fold_space,
        ], 10,
    )

    half = n_row // 2

    def routed(value, slot):
        pairs = []
        for t in range(n_tm):
            for r in range(n_row):
                target = r // 2 if (r % 2 == 0) == (slot == 0) else half + r // 2
                pairs.append((t * n_row + r, t * n_row + target))
        return lax.ppermute(value, AXES, pairs)

    first = out[0] + jnp.where(tm > 0, carry, 0.0)
    last = out[1]
    is_even = row % 2 == 0
    got_a = routed(jnp.where(is_even, first, last), 0)
    got_b = routed(jnp.where(is_even, last, first), 1)
    low = row < half
    return jnp.concatenate([jnp.where(low, got_a, got_b), jnp.where(low, got_b, got_a)], axis=0)


def solution(mesh):
    return jax.shard_map(
        on_device,
        mesh=mesh,
        in_specs=(P("tm", "row", None, None), P(), P(), P(), P()),
        out_specs=P(AXES, None),
        check_vma=False,
    )
```

```python
import jax
import jax.numpy as jnp
from jax import lax
from jax.experimental import pallas as pl
from jax.experimental.pallas import tpu as pltpu
from jax.sharding import PartitionSpec as P

F32 = jnp.float32
BF16 = jnp.bfloat16
VMEM_LIMIT = 24 * 1024 * 1024
AXES = ("tm", "row")
HALO = pl.ANY


def widen(rows, target, keep=None):
    width, channels = rows.shape
    if keep is not None:
        rows = jnp.where(keep, rows.astype(F32), 0.0).astype(BF16)
    value = rows.astype(F32)
    column = lax.broadcasted_iota(jnp.int32, (width, channels), 0)
    before = jnp.where(column == 0, 0.0, pltpu.roll(value, 1, 0))
    after = jnp.where(column == width - 1, 0.0, pltpu.roll(value, width - 1, 0))
    target[:, 0:channels] = before.astype(BF16)
    target[:, channels : 2 * channels] = rows
    target[:, 2 * channels : 3 * channels] = after.astype(BF16)


def tap_product(weight, positions):
    positions = positions.reshape(-1, weight.shape[1])
    return lax.dot_general(weight, positions, (((1,), (1,)), ((), ())), preferred_element_type=F32)


def projected(pre, bias, down_ref, f, rows):
    taps = (1,) if f % 2 == 0 else (2, 0)
    act = []
    for value in pre:
        value = value + bias
        act.append((value / (1.0 + jnp.exp(-value))).astype(BF16))
    weight = []
    for a in taps:
        for i in rows:
            parts = [down_ref[a, i % 2, dx] for dx in (0, 0, 1, 1)]
            weight.append(jnp.concatenate(parts, axis=0))
    product = jnp.dot(jnp.concatenate(weight, axis=0), jnp.concatenate(act, axis=1), preferred_element_type=F32)
    width = pre[0].shape[1]
    size = weight[0].shape[0]
    found = {}
    for n, a in enumerate(taps):
        for half in range(2):
            first = (2 * n + half) * size
            found[a, half] = product[first : first + size, half * width : (half + 1) * width]
    return found


def add_products(found, a, total_ref):
    for half in range(2):
        value = found[a, half]
        size = value.shape[0] // 2
        for dx in range(2):
            first = dx * 2 * size + half * size
            total_ref[first : first + size, :] += value[dx * size : (dx + 1) * size]


def fold(total, d_ref):
    d_ref[...] = total.T
    lanes = total.shape[0]
    count = total.shape[1] // 4
    lane = lax.broadcasted_iota(jnp.int32, (count, lanes), 1)
    result = jnp.zeros((count, lanes), F32)
    for s in range(4):
        keep = (lane // (lanes // 2) == s % 2) & ((lane // (lanes // 8)) % 2 == s // 2)
        result = result + jnp.where(keep, d_ref[pl.ds(s, count, stride=4), :], 0.0)
    return (result + pltpu.roll(result, lanes // 2, 1))[:, : lanes // 2]


def exists(side):
    if side == 2:
        return lax.axis_index("tm") > 0
    row = lax.axis_index("row")
    return row > 0 if side == 0 else row < lax.axis_size("row") - 1


def copies(pairs, sems, first=0):
    started = []
    for n, (source, target) in enumerate(pairs):
        started.append(pltpu.make_async_copy(source, target, sems.at[first + n]))
        started[-1].start()
    return started


def tap_rows(tap_row, height):
    return range(max(0, tap_row - 1), min(height, height + tap_row - 1))


def up_kernel(x_ref, up_ref, sems):
    (copy,) = copies([(x_ref.at[:, x_ref.shape[1] - 1 :], up_ref)], sems)
    copy.wait()


def send_kernel(x_ref, up_ref, dn_ref, late_ref, sems):
    for copy in copies([(x_ref.at[:, :1], dn_ref), (x_ref.at[2:], late_ref)], sems):
        copy.wait()


def relay_kernel(up, dn, out_ref, sems):
    for copy in copies([(up.at[2:], out_ref.at[:, :1]), (dn.at[2:], out_ref.at[:, 1:])], sems):
        copy.wait()


def own_kernel(
    x_ref, w_ref, bias_in, down_in, acc, weights, bias_ref, down_ref, totals, edge_weights, rows_in, staged, bias_row, wide, sems
):
    frames, height, width, channels = x_ref.shape
    order = [(a, b) for a in (2, 1, 0) for b in (1, 0, 2)]
    heavy = copies([(w_ref.at[order[0]], staged.at[order[0]])], sems, frames)
    fetch = copies([(x_ref.at[f], rows_in.at[f]) for f in range(frames)], sems)
    small = copies([(bias_in, bias_row), (down_in, down_ref)], sems, frames + 9)
    heavy += copies([(w_ref.at[order[1]], staged.at[order[1]])], sems, frames + 1)
    moved = []
    for n, (tap_time, tap_row) in enumerate(order):
        heavy[n].wait()
        if n + 2 < len(order):
            heavy += copies([(w_ref.at[order[n + 2]], staged.at[order[n + 2]])], sems, frames + n + 2)
        weights[tap_time, tap_row] = staged[tap_time, tap_row].reshape(3 * channels, channels).T
        if tap_row != 1:
            moved += copies(
                [(weights.at[tap_time, tap_row], edge_weights.at[tap_time, tap_row // 2])], sems, frames + 11 + len(moved)
            )
        if n == 0:
            for f in range(frames):
                fetch[f].wait()
                for h in range(height):
                    widen(rows_in[f, h], wide.at[h, f])
                product = tap_product(weights[tap_time, tap_row], wide[:, f])
                for h in range(height):
                    acc[h, f] = product[:, h * width : (h + 1) * width]
            continue
        count = frames - 2 + tap_time
        rows = tap_rows(tap_row, height)
        product = tap_product(weights[tap_time, tap_row], wide[rows[0] : rows[-1] + 1, :count])
        for m, h in enumerate(rows):
            for g in range(count):
                first = (m * count + g) * width
                acc[h + 1 - tap_row, g + 2 - tap_time] += product[:, first : first + width]
    for copy in small:
        copy.wait()
    bias_ref[...] = jnp.broadcast_to(bias_row[...].reshape(1, channels), (width, channels)).T
    totals[...] = jnp.zeros_like(totals)
    for f in (2, 3):
        project_rows([acc[i, f] for i in (1, 2)], f, (1, 2), bias_ref[...], down_ref, totals)
    for copy in moved:
        copy.wait()


def project_rows(pre, f, rows, bias, down_ref, totals):
    found = projected(pre, bias, down_ref, f, rows)
    add_products(found, 1 + f % 2, totals.at[f // 2])
    if f % 2 == 1:
        add_products(found, 0, totals.at[f // 2 + 1])


def earlier_kernel(x_ref, acc_in, weights, bias_ref, down_ref, totals_in, edge_ref, totals_ref, rows_in, acc, totals, wide, sems):
    frames, height, width, channels = x_ref.shape
    (fetch,) = copies([(x_ref, rows_in)], sems)
    moved = copies([(acc_in.at[side * (height - 1), 2:], edge_ref.at[side, 2:]) for side in range(2)], sems, 1)
    totals[...] = totals_in[...]
    keep = exists(2)
    fetch.wait()

    def one(n, carry):
        f, h = n // height, n % height
        widen(rows_in[f, h], wide.at[h, f], keep)
        return carry

    lax.fori_loop(0, frames * height, one, 0)
    for tap_time in (0, 1):
        for tap_row in (1, 0, 2):
            rows = tap_rows(tap_row, height)
            count = frames - tap_time
            product = tap_product(weights[tap_time, tap_row], wide[rows[0] : rows[-1] + 1, tap_time:])
            for m, h in enumerate(rows):
                for f in range(count):
                    first = (m * count + f) * width
                    target = (h + 1 - tap_row, f)
                    value = acc_in[target] if (tap_time, tap_row) == (0, 1) else acc[target]
                    acc[target] = value + product[:, first : first + width]
    moved += copies([(acc.at[side * (height - 1)], edge_ref.at[side, :2]) for side in range(2)], sems, 3)
    for f in (0, 1):
        project_rows([acc[i, f] for i in (1, 2)], f, (1, 2), bias_ref[...], down_ref, totals)
    moved += copies([(totals, totals_ref)], sems, 5)
    for copy in moved:
        copy.wait()


def rows_kernel(
    up, dn, edge_in, w_ref, totals_in, bias_in, down_in, edge_ref, totals_ref, carry_ref,
    initial, edge, weights, bias_row, down_ref, totals, sides_in, sides, d_ref, sems,
):
    width, channels = sides_in.shape[2:]
    order = [(a, side) for a in (2, 1, 0) for side in range(2)]
    brought = copies([(up.at[:, 0], sides_in.at[0])], sems, 6)
    heavy = copies([(w_ref.at[order[0]], weights.at[0])], sems)
    brought += copies([(dn.at[:, 0], sides_in.at[1])], sems, 7)
    heavy += copies([(w_ref.at[t], weights.at[n + 1]) for n, t in enumerate(order[1:3])], sems, 1)
    late = []
    for n, (tap_time, side) in enumerate(order):
        count = tap_time + 2
        if n < 2:
            brought[side].wait()
            for f in range(4):
                widen(sides_in[side, f], sides.at[side, f], exists(side))
        heavy[n].wait()
        if n + 3 < len(order):
            heavy += copies([(w_ref.at[order[n + 3]], weights.at[n + 3])], sems, n + 3)
        if n == 1:
            late = copies([(edge_in, initial), (totals_in, totals), (bias_in, bias_row), (down_in, down_ref)], sems, 8)
        product = tap_product(weights[n], sides[side, :count])
        for m in range(count):
            value = product[:, m * width : (m + 1) * width]
            if n < 2:
                edge[side, m] = value
            else:
                edge[side, m + 2 - tap_time] += value
        if n == 3:
            for copy in late:
                copy.wait()
            for s in range(2):
                for f in range(2):
                    edge[s, f] += initial[s, f]
            moved = copies([(edge.at[s, :2], edge_ref.at[s]) for s in range(2)], sems)
    bias = jnp.broadcast_to(bias_row[...].reshape(1, channels), (width, channels)).T
    for f in (2, 3):
        project_rows([edge[side, f] + initial[side, f] for side in range(2)], f, (0, 3), bias, down_ref, totals)
    moved += copies([(totals, totals_ref)], sems, 2)
    carry_ref[...] = fold(totals[2], d_ref)
    for copy in moved:
        copy.wait()


def corner_kernel(
    corner, edge_in, w_ref, totals_in, bias_in, down_in, down_bias_ref, out_ref,
    initial, edge, weights, bias_row, down_ref, totals, sides_in, sides, d_ref, sems,
):
    width, channels = sides_in.shape[2:]
    order = [(a, side) for a in range(2) for side in range(2)]
    brought = copies([(corner.at[:, 0], sides_in.at[0])], sems)
    heavy = copies([(w_ref.at[order[0]], weights.at[order[0]])], sems, 2)
    brought += copies([(corner.at[:, 1], sides_in.at[1])], sems, 1)
    heavy += copies([(w_ref.at[order[1]], weights.at[order[1]])], sems, 3)
    heavy += copies([(w_ref.at[t], weights.at[t]) for t in order[2:]], sems, 4)
    late = copies([(edge_in, initial), (totals_in, totals), (bias_in, bias_row), (down_in, down_ref)], sems, 6)
    for n, (tap_time, side) in enumerate(order):
        if n < 2:
            brought[side].wait()
            for f in range(2):
                widen(sides_in[side, f], sides.at[side, f], exists(side) & exists(2))
        heavy[n].wait()
        product = tap_product(weights[tap_time, side], sides[side, tap_time:])
        for f in range(2 - tap_time):
            value = product[:, f * width : (f + 1) * width]
            if tap_time == 0:
                edge[side, f] = value
            else:
                edge[side, f] += value
    for copy in late:
        copy.wait()
    bias = jnp.broadcast_to(bias_row[...].reshape(1, channels), (width, channels)).T
    for f in (0, 1):
        project_rows([edge[side, f] + initial[side, f] for side in range(2)], f, (0, 3), bias, down_ref, totals)
    latent_bias = down_bias_ref[...].reshape(1, -1)
    latent_bias = jnp.concatenate([latent_bias] * 4, axis=1)
    for t in range(2):
        out_ref[t] = fold(totals[t], d_ref) + latent_bias


def on_device(feature, conv_weight, conv_bias, down_weight, down_bias):
    frames, height, width, channels = feature.shape
    z = down_bias.shape[0]
    n_tm, n_row = lax.axis_size("tm"), lax.axis_size("row")
    tm, row = lax.axis_index("tm"), lax.axis_index("row")
    quarter, lanes = width // 4, 8 * z

    def shifted(value, by_tm, by_row):
        pairs = [
            (t * n_row + r, (t + by_tm) % n_tm * n_row + (r + by_row) % n_row) for t in range(n_tm) for r in range(n_row)
        ]
        return lax.ppermute(value, AXES, pairs)

    hbm_ref, halo_ref = pl.BlockSpec(memory_space=pltpu.HBM), pl.BlockSpec(memory_space=HALO)
    vmem = pl.BlockSpec(memory_space=pltpu.VMEM)

    def in_hbm(value):
        return pltpu.with_memory_space_constraint(value, pltpu.HBM)

    def call(kernel, name, units, ins, specs, outs, out_specs, scratch, copied):
        return pl.pallas_call(
            kernel,
            in_specs=specs,
            out_specs=out_specs,
            out_shape=outs,
            scratch_shapes=[*scratch, pltpu.SemaphoreType.DMA((copied,))],
            compiler_params=pltpu.CompilerParams(vmem_limit_bytes=VMEM_LIMIT),
            cost_estimate=pl.CostEstimate(
                flops=units * width * 6 * channels * channels, bytes_accessed=4_000_000, transcendentals=0
            ),
            name=name,
        )(*[in_hbm(i) if spec is hbm_ref else i for i, spec in zip(ins, specs)])

    edge_row = pltpu.VMEM((frames, 1, width, channels), BF16)
    (up_row,) = call(up_kernel, "send_up", 0, (feature,), [hbm_ref], [edge_row], [vmem], [], 1)
    up = shifted(up_row, 0, 1)
    dn, earlier = call(
        send_kernel, "send", 1, (feature, up_row), [hbm_ref, halo_ref],
        [edge_row, pltpu.VMEM((2, height, width, channels), BF16)], [vmem] * 2, [], 2,
    )
    dn = shifted(dn, 0, -1)
    earlier = shifted(earlier, 1, 0)

    down = down_weight.transpose(0, 1, 2, 4, 3)
    totals_shape = (3, lanes, width)
    *kept, edge_weights = call(
        own_kernel, "own", 90, (feature, conv_weight, conv_bias, down), [hbm_ref] * 4,
        [
            pltpu.VMEM((height, frames, channels, width), F32), pltpu.VMEM((3, 3, channels, 3 * channels), BF16),
            pltpu.VMEM((channels, width), F32), pltpu.VMEM(down.shape, BF16), pltpu.VMEM(totals_shape, F32),
            pltpu.HBM((3, 2, channels, 3 * channels), BF16),
        ],
        [vmem] * 5 + [hbm_ref],
        [
            pltpu.VMEM(feature.shape, BF16), pltpu.VMEM(conv_weight.shape, BF16), pltpu.VMEM(conv_bias.shape, F32),
            pltpu.VMEM((height, frames, width, 3 * channels), BF16),
        ], frames + 17,
    )
    edges, totals = call(
        earlier_kernel, "earlier", 30, (earlier, *kept), [halo_ref] + [vmem] * 5,
        [pltpu.HBM((2, frames, channels, width), F32), pltpu.HBM(totals_shape, F32)], [hbm_ref] * 2,
        [
            pltpu.VMEM(earlier.shape, BF16), pltpu.VMEM((height, 2, channels, width), F32), pltpu.VMEM(totals_shape, F32),
            pltpu.VMEM((height, 2, width, 3 * channels), BF16),
        ], 6,
    )
    up, dn, totals = lax.optimization_barrier((up, dn, totals))
    (corner,) = call(
        relay_kernel, "relay", 1, (up, dn), [halo_ref, halo_ref],
        [pltpu.HBM((2, 2, width, channels), BF16)], [hbm_ref], [], 2,
    )
    corner = shifted(corner, 1, 0)
    edge_shape = (2, 2, channels, width)
    small = [pltpu.VMEM(conv_bias.shape, F32), pltpu.VMEM(down.shape, BF16), pltpu.VMEM(totals_shape, F32)]
    fold_space = pltpu.VMEM((width, lanes), F32)
    edges, totals, carry = call(
        rows_kernel, "rows", 18, (up, dn, edges, edge_weights, totals, conv_bias, down), [halo_ref] * 2 + [hbm_ref] * 5,
        [pltpu.HBM(edge_shape, F32), pltpu.HBM(totals_shape, F32), jax.ShapeDtypeStruct((quarter, 4 * z), F32)],
        [hbm_ref, hbm_ref, vmem],
        [
            *[pltpu.VMEM((2, frames, channels, width), F32)] * 2, pltpu.VMEM((6, channels, 3 * channels), BF16), *small,
            pltpu.VMEM((2, frames, width, channels), BF16), pltpu.VMEM((2, frames, width, 3 * channels), BF16), fold_space,
        ], 13,
    )
    carry = shifted(carry, 1, 0)
    (out,) = call(
        corner_kernel, "corners", 6, (corner, edges, edge_weights, totals, conv_bias, down, down_bias),
        [halo_ref] + [hbm_ref] * 5 + [vmem],
        [jax.ShapeDtypeStruct((2, quarter, 4 * z), F32)], [vmem],
        [
            *[pltpu.VMEM(edge_shape, F32)] * 2, pltpu.VMEM((2, 2, channels, 3 * channels), BF16), *small,
            pltpu.VMEM((2, 2, width, channels), BF16), pltpu.VMEM((2, 2, width, 3 * channels), BF16), fold_space,
        ], 10,
    )

    half = n_row // 2

    def routed(value, slot):
        pairs = []
        for t in range(n_tm):
            for r in range(n_row):
                target = r // 2 if (r % 2 == 0) == (slot == 0) else half + r // 2
                pairs.append((t * n_row + r, t * n_row + target))
        return lax.ppermute(value, AXES, pairs)

    first = out[0] + jnp.where(tm > 0, carry, 0.0)
    last = out[1]
    is_even = row % 2 == 0
    got_a = routed(jnp.where(is_even, first, last), 0)
    got_b = routed(jnp.where(is_even, last, first), 1)
    low = row < half
    return jnp.concatenate([jnp.where(low, got_a, got_b), jnp.where(low, got_b, got_a)], axis=0)


def solution(mesh):
    return jax.shard_map(
        on_device,
        mesh=mesh,
        in_specs=(P("tm", "row", None, None), P(), P(), P(), P()),
        out_specs=P(AXES, None),
        check_vma=False,
    )
```

```python
import jax
import jax.numpy as jnp
from jax import lax
from jax.experimental import pallas as pl
from jax.experimental.pallas import tpu as pltpu
from jax.sharding import PartitionSpec as P

F32 = jnp.float32
BF16 = jnp.bfloat16
VMEM_LIMIT = 24 * 1024 * 1024
AXES = ("tm", "row")
HALO = pl.ANY


def widen(rows, target, keep=None):
    width, channels = rows.shape
    if keep is not None:
        rows = jnp.where(keep, rows.astype(F32), 0.0).astype(BF16)
    value = rows.astype(F32)
    column = lax.broadcasted_iota(jnp.int32, (width, channels), 0)
    before = jnp.where(column == 0, 0.0, pltpu.roll(value, 1, 0))
    after = jnp.where(column == width - 1, 0.0, pltpu.roll(value, width - 1, 0))
    target[:, 0:channels] = before.astype(BF16)
    target[:, channels : 2 * channels] = rows
    target[:, 2 * channels : 3 * channels] = after.astype(BF16)


def tap_product(weight, positions):
    positions = positions.reshape(-1, weight.shape[1])
    return lax.dot_general(weight, positions, (((1,), (1,)), ((), ())), preferred_element_type=F32)


def projected(pre, bias, down_ref, f, rows):
    taps = (1,) if f % 2 == 0 else (2, 0)
    act = []
    for value in pre:
        value = value + bias
        act.append((value / (1.0 + jnp.exp(-value))).astype(BF16))
    weight = []
    for a in taps:
        for i in rows:
            parts = [down_ref[a, i % 2, dx] for dx in (0, 0, 1, 1)]
            weight.append(jnp.concatenate(parts, axis=0))
    product = jnp.dot(jnp.concatenate(weight, axis=0), jnp.concatenate(act, axis=1), preferred_element_type=F32)
    width = pre[0].shape[1]
    size = weight[0].shape[0]
    found = {}
    for n, a in enumerate(taps):
        for half in range(2):
            first = (2 * n + half) * size
            found[a, half] = product[first : first + size, half * width : (half + 1) * width]
    return found


def add_products(found, a, total_ref):
    for half in range(2):
        value = found[a, half]
        size = value.shape[0] // 2
        for dx in range(2):
            first = dx * 2 * size + half * size
            total_ref[first : first + size, :] += value[dx * size : (dx + 1) * size]


def fold(total, d_ref):
    d_ref[...] = total.T
    lanes = total.shape[0]
    count = total.shape[1] // 4
    lane = lax.broadcasted_iota(jnp.int32, (count, lanes), 1)
    result = jnp.zeros((count, lanes), F32)
    for s in range(4):
        keep = (lane // (lanes // 2) == s % 2) & ((lane // (lanes // 8)) % 2 == s // 2)
        result = result + jnp.where(keep, d_ref[pl.ds(s, count, stride=4), :], 0.0)
    return (result + pltpu.roll(result, lanes // 2, 1))[:, : lanes // 2]


def exists(side):
    if side == 2:
        return lax.axis_index("tm") > 0
    row = lax.axis_index("row")
    return row > 0 if side == 0 else row < lax.axis_size("row") - 1


def copies(pairs, sems, first=0):
    started = []
    for n, (source, target) in enumerate(pairs):
        started.append(pltpu.make_async_copy(source, target, sems.at[first + n]))
        started[-1].start()
    return started


def tap_rows(tap_row, height):
    return range(max(0, tap_row - 1), min(height, height + tap_row - 1))


def up_kernel(x_ref, up_ref, sems):
    (copy,) = copies([(x_ref.at[:, x_ref.shape[1] - 1 :], up_ref)], sems)
    copy.wait()


def send_kernel(x_ref, up_ref, dn_ref, late_ref, sems):
    for copy in copies([(x_ref.at[:, :1], dn_ref), (x_ref.at[2:], late_ref)], sems):
        copy.wait()


def relay_kernel(up, dn, out_ref, sems):
    for copy in copies([(up.at[2:], out_ref.at[:, :1]), (dn.at[2:], out_ref.at[:, 1:])], sems):
        copy.wait()


def own_kernel(
    x_ref, w_ref, bias_in, down_in, acc, weights, bias_ref, down_ref, totals, edge_weights, rows_in, staged, bias_row, wide, sems
):
    frames, height, width, channels = x_ref.shape
    order = [(2, 1), (2, 0), (2, 2), (1, 0), (1, 2), (1, 1), (0, 0), (0, 2), (0, 1)]
    heavy = copies([(w_ref.at[order[0]], staged.at[order[0]])], sems, frames)
    fetch = copies([(x_ref.at[f], rows_in.at[f]) for f in range(frames)], sems)
    small = copies([(bias_in, bias_row), (down_in, down_ref)], sems, frames + 9)
    heavy += copies([(w_ref.at[order[1]], staged.at[order[1]])], sems, frames + 1)
    moved = []
    for n, (tap_time, tap_row) in enumerate(order):
        heavy[n].wait()
        if n + 2 < len(order):
            heavy += copies([(w_ref.at[order[n + 2]], staged.at[order[n + 2]])], sems, frames + n + 2)
        weights[tap_time, tap_row] = staged[tap_time, tap_row].reshape(3 * channels, channels).T
        if tap_row != 1:
            moved += copies(
                [(weights.at[tap_time, tap_row], edge_weights.at[tap_time, tap_row // 2])], sems, frames + 11 + len(moved)
            )
        if n == 0:
            for f in range(frames):
                fetch[f].wait()
                for h in range(height):
                    widen(rows_in[f, h], wide.at[h, f])
                product = tap_product(weights[tap_time, tap_row], wide[:, f])
                for h in range(height):
                    acc[h, f] = product[:, h * width : (h + 1) * width]
            continue
        count = frames - 2 + tap_time
        rows = tap_rows(tap_row, height)
        product = tap_product(weights[tap_time, tap_row], wide[rows[0] : rows[-1] + 1, :count])
        for m, h in enumerate(rows):
            for g in range(count):
                first = (m * count + g) * width
                acc[h + 1 - tap_row, g + 2 - tap_time] += product[:, first : first + width]
    for copy in small:
        copy.wait()
    bias_ref[...] = jnp.broadcast_to(bias_row[...].reshape(1, channels), (width, channels)).T
    totals[...] = jnp.zeros_like(totals)
    for f in (2, 3):
        project_rows([acc[i, f] for i in (1, 2)], f, (1, 2), bias_ref[...], down_ref, totals)
    for copy in moved:
        copy.wait()


def project_rows(pre, f, rows, bias, down_ref, totals):
    found = projected(pre, bias, down_ref, f, rows)
    add_products(found, 1 + f % 2, totals.at[f // 2])
    if f % 2 == 1:
        add_products(found, 0, totals.at[f // 2 + 1])


def earlier_kernel(x_ref, acc_in, weights, bias_ref, down_ref, totals_in, edge_ref, totals_ref, rows_in, acc, totals, wide, sems):
    frames, height, width, channels = x_ref.shape
    (fetch,) = copies([(x_ref, rows_in)], sems)
    moved = copies([(acc_in.at[side * (height - 1), 2:], edge_ref.at[side, 2:]) for side in range(2)], sems, 1)
    totals[...] = totals_in[...]
    keep = exists(2)
    fetch.wait()

    def one(n, carry):
        f, h = n // height, n % height
        widen(rows_in[f, h], wide.at[h, f], keep)
        return carry

    lax.fori_loop(0, frames * height, one, 0)
    for tap_time in (0, 1):
        for tap_row in (1, 0, 2):
            rows = tap_rows(tap_row, height)
            count = frames - tap_time
            product = tap_product(weights[tap_time, tap_row], wide[rows[0] : rows[-1] + 1, tap_time:])
            for m, h in enumerate(rows):
                for f in range(count):
                    first = (m * count + f) * width
                    target = (h + 1 - tap_row, f)
                    value = acc_in[target] if (tap_time, tap_row) == (0, 1) else acc[target]
                    acc[target] = value + product[:, first : first + width]
    moved += copies([(acc.at[side * (height - 1)], edge_ref.at[side, :2]) for side in range(2)], sems, 3)
    for f in (0, 1):
        project_rows([acc[i, f] for i in (1, 2)], f, (1, 2), bias_ref[...], down_ref, totals)
    moved += copies([(totals, totals_ref)], sems, 5)
    for copy in moved:
        copy.wait()


def rows_kernel(
    up, dn, edge_in, w_ref, totals_in, bias_in, down_in, edge, weights, bias_ref, down_ref, totals, carry_ref,
    initial, bias_row, sides_in, sides, d_ref, sems,
):
    width, channels = sides_in.shape[2:]
    order = [(a, side) for a in (2, 1, 0) for side in range(2)]
    brought = copies([(up.at[:, 0], sides_in.at[0])], sems, 6)
    heavy = copies([(w_ref.at[order[0]], weights.at[order[0]])], sems)
    brought += copies([(dn.at[:, 0], sides_in.at[1])], sems, 7)
    heavy += copies([(w_ref.at[t], weights.at[t]) for t in order[1:3]], sems, 1)
    for n, (tap_time, side) in enumerate(order):
        count = tap_time + 2
        if n < 2:
            brought[side].wait()
            for f in range(4):
                widen(sides_in[side, f], sides.at[side, f], exists(side))
        heavy[n].wait()
        if n + 3 < len(order):
            heavy += copies([(w_ref.at[order[n + 3]], weights.at[order[n + 3]])], sems, n + 3)
        if n == 1:
            late = copies([(edge_in, initial), (totals_in, totals), (bias_in, bias_row), (down_in, down_ref)], sems, 8)
        product = tap_product(weights[tap_time, side], sides[side, :count])
        for m in range(count):
            value = product[:, m * width : (m + 1) * width]
            if n < 2:
                edge[side, m] = value
            else:
                edge[side, m + 2 - tap_time] += value
    for copy in late:
        copy.wait()
    for side in range(2):
        for f in range(2):
            edge[side, f] += initial[side, f]
    bias = jnp.broadcast_to(bias_row[...].reshape(1, channels), (width, channels)).T
    bias_ref[...] = bias
    for f in (2, 3):
        project_rows([edge[side, f] + initial[side, f] for side in range(2)], f, (0, 3), bias, down_ref, totals)
    carry_ref[...] = fold(totals[2], d_ref)


def corner_kernel(
    corner, edge_in, weights, bias_ref, down_ref, totals_in, down_bias_ref, out_ref, edge, totals, sides_in, sides, d_ref, sems
):
    width = sides_in.shape[2]
    brought = copies([(corner.at[:, side], sides_in.at[side]) for side in range(2)], sems)
    totals[...] = totals_in[...]
    for tap_time in range(2):
        for side in range(2):
            if tap_time == 0:
                brought[side].wait()
                for f in range(2):
                    widen(sides_in[side, f], sides.at[side, f], exists(side) & exists(2))
            product = tap_product(weights[tap_time, side], sides[side, tap_time:])
            for f in range(2 - tap_time):
                value = product[:, f * width : (f + 1) * width]
                edge[side, f] = value + (edge_in[side, f] if tap_time == 0 else edge[side, f])
    for f in (0, 1):
        project_rows([edge[side, f] for side in range(2)], f, (0, 3), bias_ref[...], down_ref, totals)
    latent_bias = down_bias_ref[...].reshape(1, -1)
    latent_bias = jnp.concatenate([latent_bias] * 4, axis=1)
    for t in range(2):
        out_ref[t] = fold(totals[t], d_ref) + latent_bias


def on_device(feature, conv_weight, conv_bias, down_weight, down_bias):
    frames, height, width, channels = feature.shape
    z = down_bias.shape[0]
    n_tm, n_row = lax.axis_size("tm"), lax.axis_size("row")
    tm, row = lax.axis_index("tm"), lax.axis_index("row")
    quarter, lanes = width // 4, 8 * z

    def shifted(value, by_tm, by_row):
        pairs = [
            (t * n_row + r, (t + by_tm) % n_tm * n_row + (r + by_row) % n_row) for t in range(n_tm) for r in range(n_row)
        ]
        return lax.ppermute(value, AXES, pairs)

    hbm_ref, halo_ref = pl.BlockSpec(memory_space=pltpu.HBM), pl.BlockSpec(memory_space=HALO)
    vmem = pl.BlockSpec(memory_space=pltpu.VMEM)

    def in_hbm(value):
        return pltpu.with_memory_space_constraint(value, pltpu.HBM)

    def call(kernel, name, units, ins, specs, outs, out_specs, scratch, copied):
        return pl.pallas_call(
            kernel,
            in_specs=specs,
            out_specs=out_specs,
            out_shape=outs,
            scratch_shapes=[*scratch, pltpu.SemaphoreType.DMA((copied,))],
            compiler_params=pltpu.CompilerParams(vmem_limit_bytes=VMEM_LIMIT),
            cost_estimate=pl.CostEstimate(
                flops=units * width * 6 * channels * channels, bytes_accessed=4_000_000, transcendentals=0
            ),
            name=name,
        )(*[in_hbm(i) if spec is hbm_ref else i for i, spec in zip(ins, specs)])

    edge_row = pltpu.VMEM((frames, 1, width, channels), BF16)
    (up_row,) = call(up_kernel, "send_up", 0, (feature,), [hbm_ref], [edge_row], [vmem], [], 1)
    up = shifted(up_row, 0, 1)
    dn, earlier = call(
        send_kernel, "send", 1, (feature, up_row), [hbm_ref, halo_ref],
        [edge_row, pltpu.VMEM((2, height, width, channels), BF16)], [vmem] * 2, [], 2,
    )
    dn = shifted(dn, 0, -1)
    earlier = shifted(earlier, 1, 0)

    down = down_weight.transpose(0, 1, 2, 4, 3)
    totals_shape = (3, lanes, width)
    *kept, edge_weights = call(
        own_kernel, "own", 90, (feature, conv_weight, conv_bias, down), [hbm_ref] * 4,
        [
            pltpu.VMEM((height, frames, channels, width), F32), pltpu.VMEM((3, 3, channels, 3 * channels), BF16),
            pltpu.VMEM((channels, width), F32), pltpu.VMEM(down.shape, BF16), pltpu.VMEM(totals_shape, F32),
            pltpu.HBM((3, 2, channels, 3 * channels), BF16),
        ],
        [vmem] * 5 + [hbm_ref],
        [
            pltpu.VMEM(feature.shape, BF16), pltpu.VMEM(conv_weight.shape, BF16), pltpu.VMEM(conv_bias.shape, F32),
            pltpu.VMEM((height, frames, width, 3 * channels), BF16),
        ], frames + 17,
    )
    edges, totals = call(
        earlier_kernel, "earlier", 30, (earlier, *kept), [halo_ref] + [vmem] * 5,
        [pltpu.HBM((2, frames, channels, width), F32), pltpu.HBM(totals_shape, F32)], [hbm_ref] * 2,
        [
            pltpu.VMEM(earlier.shape, BF16), pltpu.VMEM((height, 2, channels, width), F32), pltpu.VMEM(totals_shape, F32),
            pltpu.VMEM((height, 2, width, 3 * channels), BF16),
        ], 6,
    )
    up, dn, totals = lax.optimization_barrier((up, dn, totals))
    (corner,) = call(
        relay_kernel, "relay", 1, (up, dn), [halo_ref, halo_ref],
        [pltpu.HBM((2, 2, width, channels), BF16)], [hbm_ref], [], 2,
    )
    corner = shifted(corner, 1, 0)
    edge_shape = (2, 2, channels, width)
    fold_space = pltpu.VMEM((width, lanes), F32)
    *kept, carry = call(
        rows_kernel, "rows", 18, (up, dn, edges, edge_weights, totals, conv_bias, down), [halo_ref] * 2 + [hbm_ref] * 5,
        [
            pltpu.VMEM((2, frames, channels, width), F32), pltpu.VMEM((3, 2, channels, 3 * channels), BF16),
            pltpu.VMEM((channels, width), F32), pltpu.VMEM(down.shape, BF16), pltpu.VMEM(totals_shape, F32),
            jax.ShapeDtypeStruct((quarter, 4 * z), F32),
        ],
        [vmem] * 6,
        [
            pltpu.VMEM((2, frames, channels, width), F32), pltpu.VMEM(conv_bias.shape, F32),
            pltpu.VMEM((2, frames, width, channels), BF16), pltpu.VMEM((2, frames, width, 3 * channels), BF16), fold_space,
        ], 12,
    )
    carry = shifted(carry, 1, 0)
    (out,) = call(
        corner_kernel, "corners", 6, (corner, *kept, down_bias), [halo_ref] + [vmem] * 6,
        [jax.ShapeDtypeStruct((2, quarter, 4 * z), F32)], [vmem],
        [
            pltpu.VMEM(edge_shape, F32), pltpu.VMEM(totals_shape, F32), pltpu.VMEM((2, 2, width, channels), BF16),
            pltpu.VMEM((2, 2, width, 3 * channels), BF16), fold_space,
        ], 2,
    )

    half = n_row // 2

    def routed(value, slot):
        pairs = []
        for t in range(n_tm):
            for r in range(n_row):
                target = r // 2 if (r % 2 == 0) == (slot == 0) else half + r // 2
                pairs.append((t * n_row + r, t * n_row + target))
        return lax.ppermute(value, AXES, pairs)

    first = out[0] + jnp.where(tm > 0, carry, 0.0)
    last = out[1]
    is_even = row % 2 == 0
    got_a = routed(jnp.where(is_even, first, last), 0)
    got_b = routed(jnp.where(is_even, last, first), 1)
    low = row < half
    return jnp.concatenate([jnp.where(low, got_a, got_b), jnp.where(low, got_b, got_a)], axis=0)


def solution(mesh):
    return jax.shard_map(
        on_device,
        mesh=mesh,
        in_specs=(P("tm", "row", None, None), P(), P(), P(), P()),
        out_specs=P(AXES, None),
        check_vma=False,
    )
```

```python
import jax
import jax.numpy as jnp
from jax import lax
from jax.experimental import pallas as pl
from jax.experimental.pallas import tpu as pltpu
from jax.sharding import PartitionSpec as P

F32 = jnp.float32
BF16 = jnp.bfloat16
VMEM_LIMIT = 24 * 1024 * 1024
AXES = ("tm", "row")
HALO = pl.ANY


def widen(rows, target, keep=None):
    width, channels = rows.shape
    if keep is not None:
        rows = jnp.where(keep, rows.astype(F32), 0.0).astype(BF16)
    value = rows.astype(F32)
    column = lax.broadcasted_iota(jnp.int32, (width, channels), 0)
    before = jnp.where(column == 0, 0.0, pltpu.roll(value, 1, 0))
    after = jnp.where(column == width - 1, 0.0, pltpu.roll(value, width - 1, 0))
    target[:, 0:channels] = before.astype(BF16)
    target[:, channels : 2 * channels] = rows
    target[:, 2 * channels : 3 * channels] = after.astype(BF16)


def tap_product(weight, positions):
    positions = positions.reshape(-1, weight.shape[1])
    return lax.dot_general(weight, positions, (((1,), (1,)), ((), ())), preferred_element_type=F32)


def projected(pre, bias, down_ref, f, rows):
    taps = (1,) if f % 2 == 0 else (2, 0)
    act = []
    for value in pre:
        value = value + bias
        act.append((value / (1.0 + jnp.exp(-value))).astype(BF16))
    weight = []
    for a in taps:
        for i in rows:
            parts = [down_ref[a, i % 2, dx] for dx in (0, 0, 1, 1)]
            weight.append(jnp.concatenate(parts, axis=0))
    product = jnp.dot(jnp.concatenate(weight, axis=0), jnp.concatenate(act, axis=1), preferred_element_type=F32)
    width = pre[0].shape[1]
    size = weight[0].shape[0]
    found = {}
    for n, a in enumerate(taps):
        for half in range(2):
            first = (2 * n + half) * size
            found[a, half] = product[first : first + size, half * width : (half + 1) * width]
    return found


def add_products(found, a, total_ref):
    for half in range(2):
        value = found[a, half]
        size = value.shape[0] // 2
        for dx in range(2):
            first = dx * 2 * size + half * size
            total_ref[first : first + size, :] += value[dx * size : (dx + 1) * size]


def fold(total, d_ref):
    d_ref[...] = total.T
    lanes = total.shape[0]
    count = total.shape[1] // 4
    lane = lax.broadcasted_iota(jnp.int32, (count, lanes), 1)
    result = jnp.zeros((count, lanes), F32)
    for s in range(4):
        keep = (lane // (lanes // 2) == s % 2) & ((lane // (lanes // 8)) % 2 == s // 2)
        result = result + jnp.where(keep, d_ref[pl.ds(s, count, stride=4), :], 0.0)
    return (result + pltpu.roll(result, lanes // 2, 1))[:, : lanes // 2]


def exists(side):
    if side == 2:
        return lax.axis_index("tm") > 0
    row = lax.axis_index("row")
    return row > 0 if side == 0 else row < lax.axis_size("row") - 1


def copies(pairs, sems, first=0):
    started = []
    for n, (source, target) in enumerate(pairs):
        started.append(pltpu.make_async_copy(source, target, sems.at[first + n]))
        started[-1].start()
    return started


def tap_rows(tap_row, height):
    return range(max(0, tap_row - 1), min(height, height + tap_row - 1))


def up_kernel(x_ref, up_ref, sems):
    (copy,) = copies([(x_ref.at[:, x_ref.shape[1] - 1 :], up_ref)], sems)
    copy.wait()


def send_kernel(x_ref, up_ref, dn_ref, late_ref, sems):
    for copy in copies([(x_ref.at[:, :1], dn_ref), (x_ref.at[2:], late_ref)], sems):
        copy.wait()


def relay_kernel(up, dn, out_ref, sems):
    for copy in copies([(up.at[2:], out_ref.at[:, :1]), (dn.at[2:], out_ref.at[:, 1:])], sems):
        copy.wait()


def own_kernel(
    x_ref, w_ref, bias_in, down_in, acc, weights, bias_ref, down_ref, totals, edge_weights, rows_in, staged, bias_row, wide, sems
):
    frames, height, width, channels = x_ref.shape
    order = [(2, 1), (2, 0), (2, 2), (1, 0), (1, 2), (1, 1), (0, 0), (0, 2), (0, 1)]
    heavy = copies([(w_ref.at[order[0]], staged.at[order[0]])], sems, frames)
    fetch = copies([(x_ref.at[f], rows_in.at[f]) for f in range(frames)], sems)
    small = copies([(bias_in, bias_row), (down_in, down_ref)], sems, frames + 9)
    heavy += copies([(w_ref.at[order[1]], staged.at[order[1]])], sems, frames + 1)
    moved = []
    for n, (tap_time, tap_row) in enumerate(order):
        heavy[n].wait()
        if n + 2 < len(order):
            heavy += copies([(w_ref.at[order[n + 2]], staged.at[order[n + 2]])], sems, frames + n + 2)
        weights[tap_time, tap_row] = staged[tap_time, tap_row].reshape(3 * channels, channels).T
        if tap_row != 1:
            moved += copies(
                [(weights.at[tap_time, tap_row], edge_weights.at[tap_time, tap_row // 2])], sems, frames + 11 + len(moved)
            )
        if n == 0:
            for f in range(frames):
                fetch[f].wait()
                for h in range(height):
                    widen(rows_in[f, h], wide.at[h, f])
                product = tap_product(weights[tap_time, tap_row], wide[:, f])
                for h in range(height):
                    acc[h, f] = product[:, h * width : (h + 1) * width]
            continue
        count = frames - 2 + tap_time
        rows = tap_rows(tap_row, height)
        product = tap_product(weights[tap_time, tap_row], wide[rows[0] : rows[-1] + 1, :count])
        for m, h in enumerate(rows):
            for g in range(count):
                first = (m * count + g) * width
                acc[h + 1 - tap_row, g + 2 - tap_time] += product[:, first : first + width]
    for copy in small:
        copy.wait()
    bias_ref[...] = jnp.broadcast_to(bias_row[...].reshape(1, channels), (width, channels)).T
    totals[...] = jnp.zeros_like(totals)
    for f in (2, 3):
        project_rows([acc[i, f] for i in (1, 2)], f, (1, 2), bias_ref[...], down_ref, totals)
    for copy in moved:
        copy.wait()


def project_rows(pre, f, rows, bias, down_ref, totals):
    found = projected(pre, bias, down_ref, f, rows)
    add_products(found, 1 + f % 2, totals.at[f // 2])
    if f % 2 == 1:
        add_products(found, 0, totals.at[f // 2 + 1])


def earlier_kernel(
    x_ref, acc, weights, bias_ref, down_ref, totals_in, edge_ref, totals_ref, edge, totals, rows_in, inner, wide, sems
):
    frames, height, width, channels = x_ref.shape
    (fetch,) = copies([(x_ref, rows_in)], sems)
    moved = copies([(acc.at[side * (height - 1), 2:], edge_ref.at[side]) for side in range(2)] + [(totals_in, totals_ref)], sems, 1)
    totals[...] = jnp.zeros_like(totals)
    keep = exists(2)
    fetch.wait()

    def one(n, carry):
        f, h = n // height, n % height
        widen(rows_in[f, h], wide.at[h, f], keep)
        return carry

    lax.fori_loop(0, frames * height, one, 0)
    for tap_time in (0, 1):
        for tap_row in (1, 0, 2):
            rows = tap_rows(tap_row, height)
            count = frames - tap_time
            product = tap_product(weights[tap_time, tap_row], wide[rows[0] : rows[-1] + 1, tap_time:])
            for m, h in enumerate(rows):
                for f in range(count):
                    first = (m * count + f) * width
                    value = product[:, first : first + width]
                    i = h + 1 - tap_row
                    ref, target = (edge, (i // (height - 1), f)) if i in (0, height - 1) else (inner, (i - 1, f))
                    ref[target] = value + (acc[i, f] if (tap_time, tap_row) == (0, 1) else ref[target])
    for f in (0, 1):
        project_rows([inner[i, f] for i in range(2)], f, (1, 2), bias_ref[...], down_ref, totals)
    for copy in moved:
        copy.wait()


def rows_kernel(
    up, dn, edge_in, w_ref, totals_in, bias_in, down_in, edge, weights, bias_ref, down_ref, totals, carry_ref,
    initial, bias_row, sides_in, sides, d_ref, sems,
):
    width, channels = sides_in.shape[2:]
    order = [(a, side) for a in (2, 1, 0) for side in range(2)]
    brought = copies([(up.at[:, 0], sides_in.at[0])], sems, 6)
    heavy = copies([(w_ref.at[order[0]], weights.at[order[0]])], sems)
    brought += copies([(dn.at[:, 0], sides_in.at[1])], sems, 7)
    heavy += copies([(w_ref.at[t], weights.at[t]) for t in order[1:3]], sems, 1)
    for n, (tap_time, side) in enumerate(order):
        count = tap_time + 2
        if n < 2:
            brought[side].wait()
            for f in range(4):
                widen(sides_in[side, f], sides.at[side, f], exists(side))
        heavy[n].wait()
        if n + 3 < len(order):
            heavy += copies([(w_ref.at[order[n + 3]], weights.at[order[n + 3]])], sems, n + 3)
        if n == 1:
            late = copies([(edge_in, initial), (totals_in, totals), (bias_in, bias_row), (down_in, down_ref)], sems, 8)
        product = tap_product(weights[tap_time, side], sides[side, :count])
        for m in range(count):
            value = product[:, m * width : (m + 1) * width]
            if n < 2:
                edge[side, m] = value
            else:
                edge[side, m + 2 - tap_time] += value
    for copy in late:
        copy.wait()
    bias = jnp.broadcast_to(bias_row[...].reshape(1, channels), (width, channels)).T
    bias_ref[...] = bias
    for f in (2, 3):
        project_rows([edge[side, f] + initial[side, f - 2] for side in range(2)], f, (0, 3), bias, down_ref, totals)
    carry_ref[...] = fold(totals[2], d_ref)


def corner_kernel(
    corner, edge_in, weights, bias_ref, down_ref, totals_in, edge_early, totals_early, down_bias_ref, out_ref,
    edge, totals, sides_in, sides, d_ref, sems,
):
    width = sides_in.shape[2]
    brought = copies([(corner.at[:, side], sides_in.at[side]) for side in range(2)], sems)
    totals[...] = totals_in[...] + totals_early[...]
    for tap_time in range(2):
        for side in range(2):
            if tap_time == 0:
                brought[side].wait()
                for f in range(2):
                    widen(sides_in[side, f], sides.at[side, f], exists(side) & exists(2))
            product = tap_product(weights[tap_time, side], sides[side, tap_time:])
            for f in range(2 - tap_time):
                value = product[:, f * width : (f + 1) * width]
                edge[side, f] = value + (edge_in[side, f] + edge_early[side, f] if tap_time == 0 else edge[side, f])
    for f in (0, 1):
        project_rows([edge[side, f] for side in range(2)], f, (0, 3), bias_ref[...], down_ref, totals)
    latent_bias = down_bias_ref[...].reshape(1, -1)
    latent_bias = jnp.concatenate([latent_bias] * 4, axis=1)
    for t in range(2):
        out_ref[t] = fold(totals[t], d_ref) + latent_bias


def on_device(feature, conv_weight, conv_bias, down_weight, down_bias):
    frames, height, width, channels = feature.shape
    z = down_bias.shape[0]
    n_tm, n_row = lax.axis_size("tm"), lax.axis_size("row")
    tm, row = lax.axis_index("tm"), lax.axis_index("row")
    quarter, lanes = width // 4, 8 * z

    def shifted(value, by_tm, by_row):
        pairs = [
            (t * n_row + r, (t + by_tm) % n_tm * n_row + (r + by_row) % n_row) for t in range(n_tm) for r in range(n_row)
        ]
        return lax.ppermute(value, AXES, pairs)

    hbm_ref, halo_ref = pl.BlockSpec(memory_space=pltpu.HBM), pl.BlockSpec(memory_space=HALO)
    vmem = pl.BlockSpec(memory_space=pltpu.VMEM)

    def in_hbm(value):
        return pltpu.with_memory_space_constraint(value, pltpu.HBM)

    def call(kernel, name, units, ins, specs, outs, out_specs, scratch, copied):
        return pl.pallas_call(
            kernel,
            in_specs=specs,
            out_specs=out_specs,
            out_shape=outs,
            scratch_shapes=[*scratch, pltpu.SemaphoreType.DMA((copied,))],
            compiler_params=pltpu.CompilerParams(vmem_limit_bytes=VMEM_LIMIT),
            cost_estimate=pl.CostEstimate(
                flops=units * width * 6 * channels * channels, bytes_accessed=4_000_000, transcendentals=0
            ),
            name=name,
        )(*[in_hbm(i) if spec is hbm_ref else i for i, spec in zip(ins, specs)])

    edge_row = pltpu.VMEM((frames, 1, width, channels), BF16)
    (up_row,) = call(up_kernel, "send_up", 0, (feature,), [hbm_ref], [edge_row], [vmem], [], 1)
    up = shifted(up_row, 0, 1)
    dn, earlier = call(
        send_kernel, "send", 1, (feature, up_row), [hbm_ref, halo_ref],
        [edge_row, pltpu.VMEM((2, height, width, channels), BF16)], [vmem] * 2, [], 2,
    )
    dn = shifted(dn, 0, -1)
    earlier = shifted(earlier, 1, 0)

    down = down_weight.transpose(0, 1, 2, 4, 3)
    totals_shape = (3, lanes, width)
    *kept, edge_weights = call(
        own_kernel, "own", 90, (feature, conv_weight, conv_bias, down), [hbm_ref] * 4,
        [
            pltpu.VMEM((height, frames, channels, width), F32), pltpu.VMEM((3, 3, channels, 3 * channels), BF16),
            pltpu.VMEM((channels, width), F32), pltpu.VMEM(down.shape, BF16), pltpu.VMEM(totals_shape, F32),
            pltpu.HBM((3, 2, channels, 3 * channels), BF16),
        ],
        [vmem] * 5 + [hbm_ref],
        [
            pltpu.VMEM(feature.shape, BF16), pltpu.VMEM(conv_weight.shape, BF16), pltpu.VMEM(conv_bias.shape, F32),
            pltpu.VMEM((height, frames, width, 3 * channels), BF16),
        ], frames + 17,
    )
    edge_shape = (2, 2, channels, width)
    edges, totals, *from_earlier = call(
        earlier_kernel, "earlier", 30, (earlier, *kept), [halo_ref] + [vmem] * 5,
        [pltpu.HBM(edge_shape, F32), pltpu.HBM(totals_shape, F32), pltpu.VMEM(edge_shape, F32), pltpu.VMEM(totals_shape, F32)],
        [hbm_ref, hbm_ref, vmem, vmem],
        [
            pltpu.VMEM(earlier.shape, BF16), pltpu.VMEM(edge_shape, F32), pltpu.VMEM((height, 2, width, 3 * channels), BF16),
        ], 4,
    )
    up, dn, totals = lax.optimization_barrier((up, dn, totals))
    (corner,) = call(
        relay_kernel, "relay", 1, (up, dn), [halo_ref, halo_ref],
        [pltpu.HBM((2, 2, width, channels), BF16)], [hbm_ref], [], 2,
    )
    corner = shifted(corner, 1, 0)
    edge_shape = (2, 2, channels, width)
    fold_space = pltpu.VMEM((width, lanes), F32)
    *kept, carry = call(
        rows_kernel, "rows", 18, (up, dn, edges, edge_weights, totals, conv_bias, down), [halo_ref] * 2 + [hbm_ref] * 5,
        [
            pltpu.VMEM((2, frames, channels, width), F32), pltpu.VMEM((3, 2, channels, 3 * channels), BF16),
            pltpu.VMEM((channels, width), F32), pltpu.VMEM(down.shape, BF16), pltpu.VMEM(totals_shape, F32),
            jax.ShapeDtypeStruct((quarter, 4 * z), F32),
        ],
        [vmem] * 6,
        [
            pltpu.VMEM(edge_shape, F32), pltpu.VMEM(conv_bias.shape, F32),
            pltpu.VMEM((2, frames, width, channels), BF16), pltpu.VMEM((2, frames, width, 3 * channels), BF16), fold_space,
        ], 12,
    )
    carry = shifted(carry, 1, 0)
    (out,) = call(
        corner_kernel, "corners", 6, (corner, *kept, *from_earlier, down_bias), [halo_ref] + [vmem] * 8,
        [jax.ShapeDtypeStruct((2, quarter, 4 * z), F32)], [vmem],
        [
            pltpu.VMEM(edge_shape, F32), pltpu.VMEM(totals_shape, F32), pltpu.VMEM((2, 2, width, channels), BF16),
            pltpu.VMEM((2, 2, width, 3 * channels), BF16), fold_space,
        ], 2,
    )

    half = n_row // 2

    def routed(value, slot):
        pairs = []
        for t in range(n_tm):
            for r in range(n_row):
                target = r // 2 if (r % 2 == 0) == (slot == 0) else half + r // 2
                pairs.append((t * n_row + r, t * n_row + target))
        return lax.ppermute(value, AXES, pairs)

    first = out[0] + jnp.where(tm > 0, carry, 0.0)
    last = out[1]
    is_even = row % 2 == 0
    got_a = routed(jnp.where(is_even, first, last), 0)
    got_b = routed(jnp.where(is_even, last, first), 1)
    low = row < half
    return jnp.concatenate([jnp.where(low, got_a, got_b), jnp.where(low, got_b, got_a)], axis=0)


def solution(mesh):
    return jax.shard_map(
        on_device,
        mesh=mesh,
        in_specs=(P("tm", "row", None, None), P(), P(), P(), P()),
        out_specs=P(AXES, None),
        check_vma=False,
    )
```

```python
import jax
import jax.numpy as jnp
from jax import lax
from jax.experimental import pallas as pl
from jax.experimental.pallas import tpu as pltpu
from jax.sharding import PartitionSpec as P

F32 = jnp.float32
BF16 = jnp.bfloat16
VMEM_LIMIT = 24 * 1024 * 1024
AXES = ("tm", "row")
HALO = pl.ANY


def widen(rows, target, keep=None):
    width, channels = rows.shape
    if keep is not None:
        rows = jnp.where(keep, rows.astype(F32), 0.0).astype(BF16)
    value = rows.astype(F32)
    column = lax.broadcasted_iota(jnp.int32, (width, channels), 0)
    before = jnp.where(column == 0, 0.0, pltpu.roll(value, 1, 0))
    after = jnp.where(column == width - 1, 0.0, pltpu.roll(value, width - 1, 0))
    target[:, 0:channels] = before.astype(BF16)
    target[:, channels : 2 * channels] = rows
    target[:, 2 * channels : 3 * channels] = after.astype(BF16)


def tap_product(weight, positions):
    positions = positions.reshape(-1, weight.shape[1])
    return lax.dot_general(weight, positions, (((1,), (1,)), ((), ())), preferred_element_type=F32)


def projected(pre, bias, down_ref, f, rows):
    taps = (1,) if f % 2 == 0 else (2, 0)
    act = []
    for value in pre:
        value = value + bias
        act.append((value / (1.0 + jnp.exp(-value))).astype(BF16))
    weight = []
    for a in taps:
        for i in rows:
            parts = [down_ref[a, i % 2, dx] for dx in (0, 0, 1, 1)]
            weight.append(jnp.concatenate(parts, axis=0))
    product = jnp.dot(jnp.concatenate(weight, axis=0), jnp.concatenate(act, axis=1), preferred_element_type=F32)
    width = pre[0].shape[1]
    size = weight[0].shape[0]
    found = {}
    for n, a in enumerate(taps):
        for half in range(2):
            first = (2 * n + half) * size
            found[a, half] = product[first : first + size, half * width : (half + 1) * width]
    return found


def add_products(found, a, total_ref):
    for half in range(2):
        value = found[a, half]
        size = value.shape[0] // 2
        for dx in range(2):
            first = dx * 2 * size + half * size
            total_ref[first : first + size, :] += value[dx * size : (dx + 1) * size]


def fold(total, d_ref):
    d_ref[...] = total.T
    lanes = total.shape[0]
    count = total.shape[1] // 4
    lane = lax.broadcasted_iota(jnp.int32, (count, lanes), 1)
    result = jnp.zeros((count, lanes), F32)
    for s in range(4):
        keep = (lane // (lanes // 2) == s % 2) & ((lane // (lanes // 8)) % 2 == s // 2)
        result = result + jnp.where(keep, d_ref[pl.ds(s, count, stride=4), :], 0.0)
    return (result + pltpu.roll(result, lanes // 2, 1))[:, : lanes // 2]


def exists(side):
    if side == 2:
        return lax.axis_index("tm") > 0
    row = lax.axis_index("row")
    return row > 0 if side == 0 else row < lax.axis_size("row") - 1


def copies(pairs, sems, first=0):
    started = []
    for n, (source, target) in enumerate(pairs):
        started.append(pltpu.make_async_copy(source, target, sems.at[first + n]))
        started[-1].start()
    return started


def tap_rows(tap_row, height):
    return range(max(0, tap_row - 1), min(height, height + tap_row - 1))


def up_kernel(x_ref, up_ref, sems):
    (copy,) = copies([(x_ref.at[:, x_ref.shape[1] - 1 :], up_ref)], sems)
    copy.wait()


def send_kernel(x_ref, up_ref, dn_ref, late_ref, sems):
    for copy in copies([(x_ref.at[:, :1], dn_ref), (x_ref.at[2:], late_ref)], sems):
        copy.wait()


def relay_kernel(up, dn, out_ref, sems):
    for copy in copies([(up.at[2:], out_ref.at[:, :1]), (dn.at[2:], out_ref.at[:, 1:])], sems):
        copy.wait()


def own_kernel(
    x_ref, w_ref, bias_in, down_in, acc, weights, bias_ref, down_ref, totals, edge_weights, rows_in, staged, bias_row, wide, sems
):
    frames, height, width, channels = x_ref.shape
    order = [(2, 1), (2, 0), (2, 2), (1, 0), (1, 2), (1, 1), (0, 0), (0, 2), (0, 1)]
    heavy = copies([(w_ref.at[order[0]], staged.at[order[0]])], sems, frames)
    fetch = copies([(x_ref.at[f], rows_in.at[f]) for f in range(frames)], sems)
    small = copies([(bias_in, bias_row), (down_in, down_ref)], sems, frames + 9)
    heavy += copies([(w_ref.at[order[1]], staged.at[order[1]])], sems, frames + 1)
    moved = []
    for n, (tap_time, tap_row) in enumerate(order):
        heavy[n].wait()
        if n + 2 < len(order):
            heavy += copies([(w_ref.at[order[n + 2]], staged.at[order[n + 2]])], sems, frames + n + 2)
        weights[tap_time, tap_row] = staged[tap_time, tap_row].reshape(3 * channels, channels).T
        if tap_row != 1:
            moved += copies(
                [(weights.at[tap_time, tap_row], edge_weights.at[tap_time, tap_row // 2])], sems, frames + 11 + len(moved)
            )
        if n == 0:
            for f in range(frames):
                fetch[f].wait()
                for h in range(height):
                    widen(rows_in[f, h], wide.at[h, f])
                product = tap_product(weights[tap_time, tap_row], wide[:, f])
                for h in range(height):
                    acc[h, f] = product[:, h * width : (h + 1) * width]
            continue
        count = frames - 2 + tap_time
        rows = tap_rows(tap_row, height)
        product = tap_product(weights[tap_time, tap_row], wide[rows[0] : rows[-1] + 1, :count])
        for m, h in enumerate(rows):
            for g in range(count):
                first = (m * count + g) * width
                acc[h + 1 - tap_row, g + 2 - tap_time] += product[:, first : first + width]
    for copy in small:
        copy.wait()
    bias_ref[...] = jnp.broadcast_to(bias_row[...].reshape(1, channels), (width, channels)).T
    totals[...] = jnp.zeros_like(totals)
    for f in (2, 3):
        project_rows([acc[i, f] for i in (1, 2)], f, (1, 2), bias_ref[...], down_ref, totals)
    for copy in moved:
        copy.wait()


def project_rows(pre, f, rows, bias, down_ref, totals):
    found = projected(pre, bias, down_ref, f, rows)
    add_products(found, 1 + f % 2, totals.at[f // 2])
    if f % 2 == 1:
        add_products(found, 0, totals.at[f // 2 + 1])


def earlier_kernel(
    x_ref, acc, weights, bias_ref, down_ref, totals_in, edge_ref, totals_ref, edge, totals, rows_in, inner, wide, sems
):
    frames, height, width, channels = x_ref.shape
    (fetch,) = copies([(x_ref, rows_in)], sems)
    moved = copies([(acc.at[side * (height - 1), 2:], edge_ref.at[side]) for side in range(2)] + [(totals_in, totals_ref)], sems, 1)
    totals[...] = jnp.zeros_like(totals)
    keep = exists(2)
    fetch.wait()

    for h in range(height):
        for f in range(frames):
            widen(rows_in[f, h], wide.at[h, f], keep)
    for tap_time in (0, 1):
        for tap_row in (1, 0, 2):
            rows = tap_rows(tap_row, height)
            count = frames - tap_time
            product = tap_product(weights[tap_time, tap_row], wide[rows[0] : rows[-1] + 1, tap_time:])
            for m, h in enumerate(rows):
                for f in range(count):
                    first = (m * count + f) * width
                    value = product[:, first : first + width]
                    i = h + 1 - tap_row
                    ref, target = (edge, (i // (height - 1), f)) if i in (0, height - 1) else (inner, (i - 1, f))
                    ref[target] = value + (acc[i, f] if (tap_time, tap_row) == (0, 1) else ref[target])
    for f in (0, 1):
        project_rows([inner[i, f] for i in range(2)], f, (1, 2), bias_ref[...], down_ref, totals)
    for copy in moved:
        copy.wait()


def rows_kernel(
    up, dn, edge_in, w_ref, totals_in, bias_in, down_in, edge, weights, bias_ref, down_ref, totals, carry_ref,
    initial, bias_row, sides_in, sides, d_ref, sems,
):
    width, channels = sides_in.shape[2:]
    order = [(a, side) for a in (2, 1, 0) for side in range(2)]
    brought = copies([(up.at[:, 0], sides_in.at[0])], sems, 6)
    heavy = copies([(w_ref.at[order[0]], weights.at[order[0]])], sems)
    brought += copies([(dn.at[:, 0], sides_in.at[1])], sems, 7)
    heavy += copies([(w_ref.at[t], weights.at[t]) for t in order[1:3]], sems, 1)
    for n, (tap_time, side) in enumerate(order):
        count = tap_time + 2
        if n < 2:
            brought[side].wait()
            for f in range(4):
                widen(sides_in[side, f], sides.at[side, f], exists(side))
        heavy[n].wait()
        if n + 3 < len(order):
            heavy += copies([(w_ref.at[order[n + 3]], weights.at[order[n + 3]])], sems, n + 3)
        if n == 1:
            late = copies([(edge_in, initial), (totals_in, totals), (bias_in, bias_row), (down_in, down_ref)], sems, 8)
        product = tap_product(weights[tap_time, side], sides[side, :count])
        for m in range(count):
            value = product[:, m * width : (m + 1) * width]
            if n < 2:
                edge[side, m] = value
            else:
                edge[side, m + 2 - tap_time] += value
    for copy in late:
        copy.wait()
    bias = jnp.broadcast_to(bias_row[...].reshape(1, channels), (width, channels)).T
    bias_ref[...] = bias
    for f in (2, 3):
        project_rows([edge[side, f] + initial[side, f - 2] for side in range(2)], f, (0, 3), bias, down_ref, totals)
    carry_ref[...] = fold(totals[2], d_ref)


def corner_kernel(
    corner, edge_in, weights, bias_ref, down_ref, totals_in, edge_early, totals_early, down_bias_ref, out_ref,
    edge, totals, sides_in, sides, d_ref, sems,
):
    width = sides_in.shape[2]
    brought = copies([(corner.at[:, side], sides_in.at[side]) for side in range(2)], sems)
    totals[...] = totals_in[...] + totals_early[...]
    for tap_time in range(2):
        for side in range(2):
            if tap_time == 0:
                brought[side].wait()
                for f in range(2):
                    widen(sides_in[side, f], sides.at[side, f], exists(side) & exists(2))
            product = tap_product(weights[tap_time, side], sides[side, tap_time:])
            for f in range(2 - tap_time):
                value = product[:, f * width : (f + 1) * width]
                edge[side, f] = value + (edge_in[side, f] + edge_early[side, f] if tap_time == 0 else edge[side, f])
    for f in (0, 1):
        project_rows([edge[side, f] for side in range(2)], f, (0, 3), bias_ref[...], down_ref, totals)
    latent_bias = down_bias_ref[...].reshape(1, -1)
    latent_bias = jnp.concatenate([latent_bias] * 4, axis=1)
    for t in range(2):
        out_ref[t] = fold(totals[t], d_ref) + latent_bias


def on_device(feature, conv_weight, conv_bias, down_weight, down_bias):
    frames, height, width, channels = feature.shape
    z = down_bias.shape[0]
    n_tm, n_row = lax.axis_size("tm"), lax.axis_size("row")
    tm, row = lax.axis_index("tm"), lax.axis_index("row")
    quarter, lanes = width // 4, 8 * z

    def shifted(value, by_tm, by_row):
        pairs = [
            (t * n_row + r, (t + by_tm) % n_tm * n_row + (r + by_row) % n_row) for t in range(n_tm) for r in range(n_row)
        ]
        return lax.ppermute(value, AXES, pairs)

    hbm_ref, halo_ref = pl.BlockSpec(memory_space=pltpu.HBM), pl.BlockSpec(memory_space=HALO)
    vmem = pl.BlockSpec(memory_space=pltpu.VMEM)

    def in_hbm(value):
        return pltpu.with_memory_space_constraint(value, pltpu.HBM)

    def call(kernel, name, units, ins, specs, outs, out_specs, scratch, copied):
        return pl.pallas_call(
            kernel,
            in_specs=specs,
            out_specs=out_specs,
            out_shape=outs,
            scratch_shapes=[*scratch, pltpu.SemaphoreType.DMA((copied,))],
            compiler_params=pltpu.CompilerParams(vmem_limit_bytes=VMEM_LIMIT),
            cost_estimate=pl.CostEstimate(
                flops=units * width * 6 * channels * channels, bytes_accessed=4_000_000, transcendentals=0
            ),
            name=name,
        )(*[in_hbm(i) if spec is hbm_ref else i for i, spec in zip(ins, specs)])

    edge_row = pltpu.VMEM((frames, 1, width, channels), BF16)
    (up_row,) = call(up_kernel, "send_up", 0, (feature,), [hbm_ref], [edge_row], [vmem], [], 1)
    up = shifted(up_row, 0, 1)
    dn, earlier = call(
        send_kernel, "send", 1, (feature, up_row), [hbm_ref, halo_ref],
        [edge_row, pltpu.VMEM((2, height, width, channels), BF16)], [vmem] * 2, [], 2,
    )
    dn = shifted(dn, 0, -1)
    earlier = shifted(earlier, 1, 0)

    down = down_weight.transpose(0, 1, 2, 4, 3)
    totals_shape = (3, lanes, width)
    *kept, edge_weights = call(
        own_kernel, "own", 90, (feature, conv_weight, conv_bias, down), [hbm_ref] * 4,
        [
            pltpu.VMEM((height, frames, channels, width), F32), pltpu.VMEM((3, 3, channels, 3 * channels), BF16),
            pltpu.VMEM((channels, width), F32), pltpu.VMEM(down.shape, BF16), pltpu.VMEM(totals_shape, F32),
            pltpu.HBM((3, 2, channels, 3 * channels), BF16),
        ],
        [vmem] * 5 + [hbm_ref],
        [
            pltpu.VMEM(feature.shape, BF16), pltpu.VMEM(conv_weight.shape, BF16), pltpu.VMEM(conv_bias.shape, F32),
            pltpu.VMEM((height, frames, width, 3 * channels), BF16),
        ], frames + 17,
    )
    edge_shape = (2, 2, channels, width)
    edges, totals, *from_earlier = call(
        earlier_kernel, "earlier", 30, (earlier, *kept), [halo_ref] + [vmem] * 5,
        [pltpu.HBM(edge_shape, F32), pltpu.HBM(totals_shape, F32), pltpu.VMEM(edge_shape, F32), pltpu.VMEM(totals_shape, F32)],
        [hbm_ref, hbm_ref, vmem, vmem],
        [
            pltpu.VMEM(earlier.shape, BF16), pltpu.VMEM(edge_shape, F32), pltpu.VMEM((height, 2, width, 3 * channels), BF16),
        ], 4,
    )
    up, dn, totals = lax.optimization_barrier((up, dn, totals))
    (corner,) = call(
        relay_kernel, "relay", 1, (up, dn), [halo_ref, halo_ref],
        [pltpu.HBM((2, 2, width, channels), BF16)], [hbm_ref], [], 2,
    )
    corner = shifted(corner, 1, 0)
    edge_shape = (2, 2, channels, width)
    fold_space = pltpu.VMEM((width, lanes), F32)
    *kept, carry = call(
        rows_kernel, "rows", 18, (up, dn, edges, edge_weights, totals, conv_bias, down), [halo_ref] * 2 + [hbm_ref] * 5,
        [
            pltpu.VMEM((2, frames, channels, width), F32), pltpu.VMEM((3, 2, channels, 3 * channels), BF16),
            pltpu.VMEM((channels, width), F32), pltpu.VMEM(down.shape, BF16), pltpu.VMEM(totals_shape, F32),
            jax.ShapeDtypeStruct((quarter, 4 * z), F32),
        ],
        [vmem] * 6,
        [
            pltpu.VMEM(edge_shape, F32), pltpu.VMEM(conv_bias.shape, F32),
            pltpu.VMEM((2, frames, width, channels), BF16), pltpu.VMEM((2, frames, width, 3 * channels), BF16), fold_space,
        ], 12,
    )
    carry = shifted(carry, 1, 0)
    (out,) = call(
        corner_kernel, "corners", 6, (corner, *kept, *from_earlier, down_bias), [halo_ref] + [vmem] * 8,
        [jax.ShapeDtypeStruct((2, quarter, 4 * z), F32)], [vmem],
        [
            pltpu.VMEM(edge_shape, F32), pltpu.VMEM(totals_shape, F32), pltpu.VMEM((2, 2, width, channels), BF16),
            pltpu.VMEM((2, 2, width, 3 * channels), BF16), fold_space,
        ], 2,
    )

    half = n_row // 2

    def routed(value, slot):
        pairs = []
        for t in range(n_tm):
            for r in range(n_row):
                target = r // 2 if (r % 2 == 0) == (slot == 0) else half + r // 2
                pairs.append((t * n_row + r, t * n_row + target))
        return lax.ppermute(value, AXES, pairs)

    first = out[0] + jnp.where(tm > 0, carry, 0.0)
    last = out[1]
    is_even = row % 2 == 0
    got_a = routed(jnp.where(is_even, first, last), 0)
    got_b = routed(jnp.where(is_even, last, first), 1)
    low = row < half
    return jnp.concatenate([jnp.where(low, got_a, got_b), jnp.where(low, got_b, got_a)], axis=0)


def solution(mesh):
    return jax.shard_map(
        on_device,
        mesh=mesh,
        in_specs=(P("tm", "row", None, None), P(), P(), P(), P()),
        out_specs=P(AXES, None),
        check_vma=False,
    )
```
